512 devices in a mesh: dom: 64 (over z, y), rep: 8 (over x, core).
Axes of the slice: x: 4, y: 4, z: 16, core: 2. Of those that a mesh axis runs over, the one named last changes fastest.
Arguments:
- entity: float32 [32768, 400], P('dom'), may hold values from -2 to 2
- adagrad_state: float32 [32768], P('dom'), may hold values from 0.01 to 4
- relation: float32 [237, 400], replicated, may hold values from 0.25 to 1.75
- src_rows: int32 [64, 8, 64, 8], P('dom', 'rep'), may hold values from 0 to 511
- dst_rows: int32 [64, 8, 64, 8], P('dom', 'rep'), may hold values from 0 to 511
- rel_ids: int32 [64, 8, 64, 8], P('dom', 'rep'), may hold values from 0 to 236
- bucket_counts: int32 [64, 8, 64], P('dom', 'rep'), may hold values from 1 to 8, as said below
- noise_rows: int32 [64, 8, 512], P('dom', 'rep'), may hold values from 0 to 511
Outputs:
- new_entity: float32 [32768, 400], P('dom')
- new_state: float32 [32768], P('dom')
The draws below stay inside these ranges and needn't reach their ends.
Inputs may be any that keep to these rules, and one draw needn't show every extreme that they name: `bucket_counts`: in every draw some destination partition has all 8 slots live in its bucket on every device, and every device has some full bucket. `noise_rows`: noise entities may repeat.
All inputs are finite; a program needn't handle non-finite values.
Results may differ from the reference program's by a relative error of at most 0.0001.
Values sent between devices are 32-bit elements; how exact they have to be, the bound alone decides.
No kernel may reach another device: no remote copies, remote signals or barrier semaphores. Data moves between devices by JAX's collectives and lax.ppermute only.
A program may use at most 64 MiB of HBM per device.

```python
import math
import jax
import jax.numpy as jnp
import numpy as np
from jax import lax

D = 400
REL = 237
NEG = 512
ENT_DEV = 512
CAP = 8
BUCKETS = 64
REPS = 8
NEG_DEV = 8
ENTITIES = 32768


def draw_bucket_counts(key, part):
    key_counts, key_owner, key_fill = jax.random.split(key, 3)
    counts = jax.random.randint(key_counts, (BUCKETS, REPS, BUCKETS), 1, CAP + 1)
    busy_owner = jax.random.randint(key_owner, (), 0, BUCKETS)
    own_full = jax.random.randint(key_fill, (BUCKETS, REPS, 1), 0, BUCKETS)
    column = jnp.arange(BUCKETS)[None, None, :]
    filled = jnp.logical_or(column == busy_owner, column == own_full)
    return jnp.where(filled, CAP, counts).astype(jnp.int32)


def place_ends(values, rng, low, high):
    longest = values.shape.index(max(values.shape))
    spots = []
    for shift in (0, 1):
        where = [jax.random.randint(jax.random.fold_in(rng, axis), (), 0, length) for axis, length in enumerate(values.shape)]
        where[longest] = (where[longest] + shift) % values.shape[longest]
        spots.append(tuple(where))
    return values.at[spots[0]].set(low).at[spots[1]].set(high)


def steps_of(key, dims, shards, least, top_value):
    def one(axis_at, parts):
        steps = jax.random.uniform(jax.random.fold_in(jax.random.fold_in(key, 6), axis_at), (parts,), jnp.float32, least / len(shards), top_value / len(shards))
        return jnp.repeat(jnp.exp(steps), dims[axis_at] // parts).reshape((-1,) + (1,) * (len(dims) - axis_at - 1))

    level = one(*shards[0])
    for cut in shards[1:]:
        level = level * one(*cut)
    return level


def rank_table(amount, skew):
    weights = [(1 << 20) // math.isqrt(rank ** skew) + 1 for rank in range(1, amount + 1)]
    deviation = 1 + sum(weights) // (1 << 30)
    return np.cumsum(np.array([max(1, weight // deviation) for weight in weights]))


def ranked(rng, shape, number_of, lean):
    table = rank_table(number_of, lean)
    ticket = jax.random.randint(jax.random.fold_in(rng, 1), shape, 0, int(table[number_of - 1]))
    rank = jnp.searchsorted(jnp.asarray(table, jnp.int32), ticket, side="right")
    return jax.random.permutation(jax.random.fold_in(rng, 2), number_of)[rank].astype(jnp.int32)


def noise(own_key, extent, deviation, most, cuts=(), kind=jnp.bfloat16):
    array = deviation * jax.random.normal(own_key, extent, jnp.float32)
    if cuts:
        array = array * steps_of(own_key, extent, cuts, -0.22, 0.18)
    return jnp.clip(array, -most, most).astype(kind)


def setup_inputs(seed: int = 0) -> dict:
    key_of = jax.random.split(jax.random.key(seed), 9)
    entity = noise(key_of[0], (ENTITIES, D), 0.3, 2.0, ((0, 64),), jnp.float32)
    adagrad_state = jnp.clip(jnp.exp(math.log(4.0) - 5.9914646 * jax.random.uniform(key_of[1], (ENTITIES,), jnp.float32) ** steps_of(key_of[1], (ENTITIES,), ((0, 64),), -0.2, 0.2)), 0.01, 4.0)
    relation = jnp.clip(1.0 + 0.15 * jax.random.normal(key_of[2], (REL, D), jnp.float32), 0.25, 1.75)
    src_rows = place_ends(jax.random.randint(key_of[3], (BUCKETS, REPS, BUCKETS, CAP), 0, ENT_DEV), jax.random.fold_in(key_of[3], 1), 0, ENT_DEV - 1).astype(jnp.int32)
    dst_rows = place_ends(jax.random.randint(key_of[4], (BUCKETS, REPS, BUCKETS, CAP), 0, ENT_DEV), jax.random.fold_in(key_of[4], 1), 0, ENT_DEV - 1).astype(jnp.int32)
    rel_ids = place_ends(ranked(key_of[5], (BUCKETS, REPS, BUCKETS, CAP), REL, 2), jax.random.fold_in(key_of[5], 3), 0, REL - 1).astype(jnp.int32)
    bucket_counts = draw_bucket_counts(jax.random.fold_in(key_of[8], 71), 0)
    noise_rows = place_ends(jax.random.randint(key_of[7], (BUCKETS, REPS, NEG), 0, ENT_DEV), jax.random.fold_in(key_of[7], 1), 0, ENT_DEV - 1).astype(jnp.int32)
    return dict(entity=entity, adagrad_state=adagrad_state, relation=relation, src_rows=src_rows, dst_rows=dst_rows, rel_ids=rel_ids, bucket_counts=bucket_counts, noise_rows=noise_rows)


LEARN_RATE = 0.3

def reference(entity, adagrad_state, relation, src_rows, dst_rows, rel_ids, bucket_counts, noise_rows):
    highest = lax.Precision.HIGHEST
    slot_index = jnp.arange(CAP, dtype=jnp.int32)
    slot_live = (slot_index[None, None, None, :] < bucket_counts[:, :, :, None]).astype(jnp.float32)
    source_base = (jnp.arange(BUCKETS, dtype=jnp.int32) * ENT_DEV)[:, None, None, None]
    owner_base = (jnp.arange(BUCKETS, dtype=jnp.int32) * ENT_DEV)[None, None, :, None]
    source_ids = (src_rows + source_base).astype(jnp.int32)
    target_ids = (dst_rows + owner_base).astype(jnp.int32)
    noise_base = jnp.arange(NEG, dtype=jnp.int32) // NEG_DEV * ENT_DEV
    noise_ids = (noise_rows + noise_base[None, None, :]).astype(jnp.int32)
    block_rows = BUCKETS * CAP
    blocks_count = BUCKETS * REPS
    blocks = (source_ids.reshape(blocks_count, block_rows), target_ids.reshape(blocks_count, block_rows), rel_ids.reshape(blocks_count, block_rows), slot_live.reshape(blocks_count, block_rows), noise_ids.reshape(blocks_count, NEG))

    def accumulate(grad, block):
        source_blk, target_blk, relate_blk, live_blk, noise_blk = block
        source_emb = entity[source_blk]
        target_emb = entity[target_blk]
        rel_rows = relation[relate_blk]
        noise_emb = entity[noise_blk]
        query = source_emb * rel_rows
        positive = lax.optimization_barrier(jnp.sum(query * target_emb, axis=1))
        negative = jnp.dot(query, noise_emb.T, precision=highest, preferred_element_type=jnp.float32)
        pos_coef = -jax.nn.sigmoid(-positive) * live_blk
        noise_coef = jax.nn.sigmoid(negative) * live_blk[:, None]
        noise_back = jnp.dot(noise_coef, noise_emb, precision=highest, preferred_element_type=jnp.float32)
        source_grad = rel_rows * (pos_coef[:, None] * target_emb + noise_back)
        target_grad = pos_coef[:, None] * query
        noise_grad = jnp.dot(noise_coef.T, query, precision=highest, preferred_element_type=jnp.float32)
        grad = grad.at[source_blk].add(source_grad)
        grad = grad.at[target_blk].add(target_grad)
        grad = grad.at[noise_blk].add(noise_grad)
        return (grad, None)
    grad, unused = lax.scan(accumulate, jnp.zeros(entity.shape, jnp.float32), blocks)
    new_state = adagrad_state + lax.optimization_barrier(jnp.mean(grad * grad, axis=1))
    new_entity = entity - LEARN_RATE * grad / jnp.sqrt(new_state)[:, None]
    return (new_entity, new_state)
```

```python
import functools

import jax
import jax.numpy as jnp
from jax import lax
from jax.experimental import pallas as pl
from jax.experimental.pallas import tpu as pltpu
from jax.sharding import Mesh
from jax.sharding import PartitionSpec as P

LEARN_RATE = 0.3
F32 = jnp.float32
BF16 = jnp.bfloat16
NN = (((1,), (0,)), ((), ()))
NT = (((1,), (1,)), ((), ()))


def round_up(value, unit):
    return -(-value // unit) * unit


def one_hot(row, rows):
    place = lax.broadcasted_iota(jnp.int32, (rows, row.shape[1]), 0)
    return (place == row).astype(F32).astype(BF16)


def split(x, terms):
    out = []
    for _ in range(terms):
        part = x.astype(BF16)
        out.append(part)
        x = x - part.astype(F32)
    return out


def mul(a, b, dims=NN):
    return lax.dot_general(a, b, dims, preferred_element_type=F32)


def pick(x, hot, dims=NN, terms=3):
    parts = split(x, terms)
    out = mul(parts[-1], hot, dims)
    for part in parts[-2::-1]:
        out = out + mul(part, hot, dims)
    return out


def product(a, b, dims=NN):
    a_high, a_low = split(a, 2)
    b_high, b_low = split(b, 2)
    return mul(a_low, b_high, dims) + mul(a_high, b_low, dims) + mul(a_high, b_high, dims)


def with_rows(x, extra, width):
    rest = width - x.shape[0]
    place = lax.broadcasted_iota(jnp.int32, (rest, x.shape[1]), 0)
    block = jnp.zeros((rest, x.shape[1]), F32)
    for i, row in enumerate(extra):
        block = jnp.where(place == i, row, block)
    return jnp.concatenate([x, block], axis=0)


def put_messages(msg_ref, rows, nz, ny):
    slots = msg_ref.shape[1]
    for y in range(ny):
        for z in range(nz):
            at = (y * nz + z) * slots
            msg_ref[z * ny + y] = rows[at : at + slots]


def query_kernel(nz, ny, et_ref, relt_ref, src_ref, rel_ref, dst_ref, live_ref, qt_ref, relation_ref, msg_ref):
    source = pick(et_ref[...], one_hot(src_ref[...], et_ref.shape[1]))
    relation = pick(relt_ref[...], one_hot(rel_ref[...], relt_ref.shape[1]))
    query = source * relation
    qt_ref[...] = query
    relation_ref[...] = relation
    full = with_rows(query, [dst_ref[...].astype(F32), live_ref[...]], msg_ref.shape[2])
    put_messages(msg_ref, full.T, nz, ny)


def owner_kernel(msg_ref, et_ref, grad_ref):
    features, rows = et_ref.shape
    full = msg_ref[...].reshape(-1, msg_ref.shape[2]).T
    query = full[:features]
    hot = one_hot(full[features : features + 1].astype(jnp.int32), rows)
    live = full[features + 1 : features + 2]
    target = pick(et_ref[...], hot)
    positive = jnp.sum(query * target, axis=0, keepdims=True)
    coef = -jax.nn.sigmoid(-positive) * live
    grad_ref[...] = pick(coef * query, hot, NT, 2)


def table_kernel(table_ref, ids_ref, out_ref, got_ref):
    nz, fs, rows = table_ref.shape
    devices = out_ref.shape[0]
    slots = ids_ref.shape[2] // (2 * devices)
    span = nz * slots

    def fetch(z, carry):
        got_ref[z] = pick(table_ref[z], one_hot(ids_ref[z], rows))
        return carry

    lax.fori_loop(0, nz, fetch, 0)
    lane = lax.broadcasted_iota(jnp.int32, (8, span), 1) // slots

    def turn(f8, carry):
        at = pl.ds(pl.multiple_of(f8 * 8, 8), 8)
        for kind in range(2):
            for tile in range(devices // nz):
                start = (kind * devices + tile * nz) * slots
                v = [got_ref[z, at, start : start + span] for z in range(nz)]
                k = nz // 2
                while k:
                    low = (lane & k) == 0
                    w = list(v)
                    for i in range(nz):
                        if not i & k:
                            a, b = v[i], v[i + k]
                            w[i] = jnp.where(low, a, pltpu.roll(b, k * slots, 1))
                            w[i + k] = jnp.where(low, pltpu.roll(a, span - k * slots, 1), b)
                    v = w
                    k //= 2
                for i in range(nz):
                    out_ref[tile * nz + i, at, kind * span : (kind + 1) * span] = v[i]
        return carry

    lax.fori_loop(0, fs // 8, turn, 0)


def lanes_of(got_ref, kind, ny, features):
    devices, fs, lanes = got_ref.shape
    span = lanes // 2
    blocks = []
    per = devices // ny
    for y in range(ny):
        block = got_ref[y * per : (y + 1) * per, :, kind * span : (kind + 1) * span]
        blocks.append(block.reshape(per * fs, span)[:features])
    return jnp.concatenate(blocks, axis=1)


def noise_kernel(nz, ny, got_ref, qt_ref, live_ref, ids_ref, coef_ref, msg_ref):
    features = qt_ref.shape[0]
    noise = lanes_of(got_ref, 0, ny, features)
    query = qt_ref[...]
    scores = product(noise.T, query)
    coef = jax.nn.sigmoid(scores) * live_ref[...]
    coef_ref[...] = coef
    grad = product(query, coef, NT)
    full = with_rows(grad, [ids_ref[...].astype(F32)], msg_ref.shape[2])
    put_messages(msg_ref, full.T, nz, ny)


def source_kernel(ny, got_ref, qt_ref, relation_ref, live_ref, src_ref, coef_ref, owned_ref, out_ref):
    features = qt_ref.shape[0]
    noise = lanes_of(got_ref, 0, ny, features)
    target = lanes_of(got_ref, 1, ny, features)
    back = product(noise, coef_ref[...])
    positive = jnp.sum(qt_ref[...] * target, axis=0, keepdims=True)
    coef = -jax.nn.sigmoid(-positive) * live_ref[...]
    grad = relation_ref[...] * (coef * target + back)
    hot = one_hot(src_ref[...], owned_ref.shape[1])
    out_ref[...] = owned_ref[...] + pick(grad, hot, NT, 2)


def scatter_kernel(msg_ref, early_ref, out_ref):
    features, rows = early_ref.shape
    reps, fs, _ = out_ref.shape
    full = msg_ref[...].reshape(-1, msg_ref.shape[2]).T
    hot = one_hot(full[features : features + 1].astype(jnp.int32), rows)
    grad = early_ref[...] + pick(full[:features], hot, NT, 2)
    rest = reps * fs - features
    if rest:
        grad = jnp.concatenate([grad, jnp.zeros((rest, rows), F32)], axis=0)
    out_ref[...] = grad.reshape(reps, fs, rows)


def update_kernel(grad_ref, et_ref, state_ref, entity_ref, new_state_ref):
    features, rows = et_ref.shape
    grad = grad_ref[...].reshape(-1, rows)[:features]
    state = state_ref[...] + jnp.sum(grad * grad, axis=0, keepdims=True) * (1.0 / features)
    new_state_ref[...] = state
    entity_ref[...] = et_ref[...] - LEARN_RATE * grad / jnp.sqrt(state)


def call(kernel, outs, *args, scratch=(), flops=0):
    shapes = [jax.ShapeDtypeStruct(shape, F32) for shape in outs]
    moved = sum(4 * a.size for a in args) + sum(4 * s.size for s in shapes)
    return pl.pallas_call(
        kernel,
        out_shape=shapes,
        scratch_shapes=list(scratch),
        cost_estimate=pl.CostEstimate(flops=flops, bytes_accessed=moved, transcendentals=0),
        compiler_params=pltpu.CompilerParams(vmem_limit_bytes=48 << 20),
    )(*args)


def per_device(entity, adagrad_state, relation, src_rows, dst_rows, rel_ids, bucket_counts, noise_rows):
    nz, ny, reps = lax.axis_size("z"), lax.axis_size("y"), lax.axis_size("rep")
    rows, features = entity.shape
    slots = src_rows.shape[3]
    parts = nz * ny
    edges = parts * slots
    fs = round_up(features, reps * 8) // reps
    width = round_up(features + 2, 128)

    def ordered(ids):
        return ids.reshape(nz, ny, slots).transpose(1, 0, 2)

    et = entity.T
    padded = jnp.pad(et, ((0, reps * fs - features), (0, 0)))
    mine = lax.dynamic_slice_in_dim(padded, lax.axis_index("rep") * fs, fs, 0)
    table = lax.all_gather(mine, "z")

    src = ordered(src_rows).reshape(1, edges)
    rel = ordered(rel_ids).reshape(1, edges)
    dst = ordered(dst_rows)
    noise = ordered(noise_rows)
    live = (jnp.arange(slots, dtype=jnp.int32) < bucket_counts.reshape(nz, ny).T[:, :, None]).astype(F32)
    live = live.reshape(1, edges)

    wanted = jnp.stack([noise.reshape(ny, -1), dst.reshape(ny, -1)], axis=1)
    wanted = jnp.broadcast_to(wanted[:, None], (ny, reps) + wanted.shape[1:])
    asked = lax.all_to_all(
        wanted.reshape(ny * reps, 2, nz * slots), ("y", "rep"), split_axis=0, concat_axis=0, tiled=True
    )
    asked = asked.reshape(ny * reps, 2, nz, slots).transpose(2, 1, 0, 3).reshape(nz, 1, -1)

    dst = dst.reshape(1, edges)
    noise = noise.reshape(1, edges)
    relt = jnp.pad(relation.T, ((0, 0), (0, round_up(relation.shape[0], 128) - relation.shape[0])))
    dense = (features, rows)
    unit = 2 * edges * features * rows
    qt, relation_rows, queries = call(
        functools.partial(query_kernel, nz, ny),
        [(features, edges), (features, edges), (parts, slots, width)],
        et, relt, src, rel, dst, live,
        flops=5 * unit,
    )
    queries = lax.all_to_all(queries, ("z", "y"), split_axis=0, concat_axis=0, tiled=True)
    (owned,) = call(owner_kernel, [dense], queries, et, flops=5 * unit)
    (found,) = call(
        table_kernel,
        [(ny * reps, fs, 2 * nz * slots)],
        table, asked,
        scratch=[pltpu.VMEM((nz, fs, 2 * ny * reps * slots), F32)],
        flops=8 * unit,
    )
    got = lax.all_to_all(found, ("y", "rep"), split_axis=0, concat_axis=0, tiled=True)
    coef, noise_grads = call(
        functools.partial(noise_kernel, nz, ny),
        [(edges, edges), (parts, slots, width)],
        got, qt, live, noise,
        flops=6 * unit,
    )
    noise_grads = lax.all_to_all(noise_grads, ("z", "y"), split_axis=0, concat_axis=0, tiled=True)
    (early,) = call(
        functools.partial(source_kernel, ny),
        [dense],
        got, qt, relation_rows, live, src, coef, owned,
        flops=5 * unit,
    )
    (partial,) = call(scatter_kernel, [(reps, fs, rows)], noise_grads, early, flops=2 * unit)
    shares = lax.all_to_all(partial, "rep", split_axis=0, concat_axis=0, tiled=True)
    summed = lax.all_gather(jnp.sum(shares, axis=0), "rep")
    new_entity, new_state = call(
        update_kernel, [dense, (1, rows)], summed, et, adagrad_state.reshape(1, rows)
    )
    return new_entity.T, new_state.reshape(rows)


def solution(mesh):
    dom, reps = mesh.devices.shape
    ny = 4 if dom >= 16 else 2
    split_mesh = Mesh(mesh.devices.reshape(dom // ny, ny, reps), ("z", "y", "rep"))
    zy = ("z", "y")
    return jax.shard_map(
        per_device,
        mesh=split_mesh,
        in_specs=(
            P(zy, None),
            P(zy),
            P(),
            P(zy, "rep", None, None),
            P(zy, "rep", None, None),
            P(zy, "rep", None, None),
            P(zy, "rep", None),
            P(zy, "rep", None),
        ),
        out_specs=(P(zy, None), P(zy)),
        check_vma=False,
    )
```

```python
import functools

import jax
import jax.numpy as jnp
from jax import lax
from jax.experimental import pallas as pl
from jax.experimental.pallas import tpu as pltpu
from jax.sharding import Mesh
from jax.sharding import PartitionSpec as P

LEARN_RATE = 0.3
F32 = jnp.float32
BF16 = jnp.bfloat16
NN = (((1,), (0,)), ((), ()))
NT = (((1,), (1,)), ((), ()))


def round_up(value, unit):
    return -(-value // unit) * unit


def one_hot(row, rows):
    place = lax.broadcasted_iota(jnp.int32, (rows, row.shape[1]), 0)
    return (place == row).astype(F32).astype(BF16)


def split(x, terms):
    out = []
    for _ in range(terms):
        part = x.astype(BF16)
        out.append(part)
        x = x - part.astype(F32)
    return out


def mul(a, b, dims=NN):
    return lax.dot_general(a, b, dims, preferred_element_type=F32)


def pick(x, hot, dims=NN, terms=3):
    n = x.shape[0]
    parts = [part.astype(F32) for part in split(x, terms)]
    out = mul(jnp.concatenate(parts, axis=0).astype(BF16), hot, dims)
    return sum(out[i * n : (i + 1) * n] for i in range(terms - 1, -1, -1))


def product(a, b, dims=NN):
    a_high, a_low = split(a, 2)
    b_high, b_low = split(b, 2)
    return mul(a_low, b_high, dims) + mul(a_high, b_low, dims) + mul(a_high, b_high, dims)


def with_rows(x, extra, width):
    rest = width - x.shape[0]
    place = lax.broadcasted_iota(jnp.int32, (rest, x.shape[1]), 0)
    block = jnp.zeros((rest, x.shape[1]), F32)
    for i, row in enumerate(extra):
        block = jnp.where(place == i, row, block)
    return jnp.concatenate([x, block], axis=0)


def put_messages(msg_ref, rows, nz, ny):
    slots = msg_ref.shape[1]
    for y in range(ny):
        for z in range(nz):
            at = (y * nz + z) * slots
            msg_ref[z * ny + y] = rows[at : at + slots]


def query_kernel(nz, ny, et_ref, relt_ref, src_ref, rel_ref, dst_ref, live_ref, qt_ref, relation_ref, msg_ref):
    source = pick(et_ref[...], one_hot(src_ref[...], et_ref.shape[1]))
    relation = pick(relt_ref[...], one_hot(rel_ref[...], relt_ref.shape[1]))
    query = source * relation
    qt_ref[...] = query
    relation_ref[...] = relation
    full = with_rows(query, [dst_ref[...].astype(F32), live_ref[...]], msg_ref.shape[2])
    put_messages(msg_ref, full.T, nz, ny)


def owner_kernel(msg_ref, et_ref, grad_ref):
    features, rows = et_ref.shape
    full = msg_ref[...].reshape(-1, msg_ref.shape[2]).T
    query = full[:features]
    hot = one_hot(full[features : features + 1].astype(jnp.int32), rows)
    live = full[features + 1 : features + 2]
    target = pick(et_ref[...], hot)
    positive = jnp.sum(query * target, axis=0, keepdims=True)
    coef = -jax.nn.sigmoid(-positive) * live
    grad_ref[...] = pick(coef * query, hot, NT, 2)


def table_kernel(table_ref, ids_ref, out_ref, got_ref):
    nz, fs, rows = table_ref.shape
    devices = out_ref.shape[0]
    slots = ids_ref.shape[2] // (2 * devices)
    span = nz * slots

    def fetch(z, carry):
        got_ref[z] = pick(table_ref[z], one_hot(ids_ref[z], rows))
        return carry

    lax.fori_loop(0, nz, fetch, 0, unroll=4)
    lane = lax.broadcasted_iota(jnp.int32, (8, span), 1) // slots

    def turn(f8, carry):
        at = pl.ds(pl.multiple_of(f8 * 8, 8), 8)
        for kind in range(2):
            for tile in range(devices // nz):
                start = (kind * devices + tile * nz) * slots
                v = [got_ref[z, at, start : start + span] for z in range(nz)]
                k = nz // 2
                while k:
                    low = (lane & k) == 0
                    w = list(v)
                    for i in range(nz):
                        if not i & k:
                            a, b = v[i], v[i + k]
                            w[i] = jnp.where(low, a, pltpu.roll(b, k * slots, 1))
                            w[i + k] = jnp.where(low, pltpu.roll(a, span - k * slots, 1), b)
                    v = w
                    k //= 2
                for i in range(nz):
                    out_ref[tile * nz + i, at, kind * span : (kind + 1) * span] = v[i]
        return carry

    lax.fori_loop(0, fs // 8, turn, 0)


def lanes_of(got_ref, kind, ny, features):
    devices, fs, lanes = got_ref.shape
    span = lanes // 2
    blocks = []
    per = devices // ny
    for y in range(ny):
        block = got_ref[y * per : (y + 1) * per, :, kind * span : (kind + 1) * span]
        blocks.append(block.reshape(per * fs, span)[:features])
    return jnp.concatenate(blocks, axis=1)


def noise_kernel(nz, ny, got_ref, qt_ref, live_ref, ids_ref, coef_ref, msg_ref):
    features = qt_ref.shape[0]
    noise = lanes_of(got_ref, 0, ny, features)
    query = qt_ref[...]
    scores = product(noise.T, query)
    coef = jax.nn.sigmoid(scores) * live_ref[...]
    coef_ref[...] = coef
    grad = product(query, coef, NT)
    full = with_rows(grad, [ids_ref[...].astype(F32)], msg_ref.shape[2])
    put_messages(msg_ref, full.T, nz, ny)


def source_kernel(ny, got_ref, qt_ref, relation_ref, live_ref, src_ref, coef_ref, owned_ref, out_ref):
    features = qt_ref.shape[0]
    noise = lanes_of(got_ref, 0, ny, features)
    target = lanes_of(got_ref, 1, ny, features)
    back = product(noise, coef_ref[...])
    positive = jnp.sum(qt_ref[...] * target, axis=0, keepdims=True)
    coef = -jax.nn.sigmoid(-positive) * live_ref[...]
    grad = relation_ref[...] * (coef * target + back)
    hot = one_hot(src_ref[...], owned_ref.shape[1])
    out_ref[...] = owned_ref[...] + pick(grad, hot, NT, 2)


def scatter_kernel(msg_ref, early_ref, out_ref):
    features, rows = early_ref.shape
    reps, fs, _ = out_ref.shape
    full = msg_ref[...].reshape(-1, msg_ref.shape[2]).T
    hot = one_hot(full[features : features + 1].astype(jnp.int32), rows)
    grad = early_ref[...] + pick(full[:features], hot, NT, 2)
    rest = reps * fs - features
    if rest:
        grad = jnp.concatenate([grad, jnp.zeros((rest, rows), F32)], axis=0)
    out_ref[...] = grad.reshape(reps, fs, rows)


def update_kernel(grad_ref, et_ref, state_ref, entity_ref, new_state_ref):
    features, rows = et_ref.shape
    grad = grad_ref[...].reshape(-1, rows)[:features]
    state = state_ref[...] + jnp.sum(grad * grad, axis=0, keepdims=True) * (1.0 / features)
    new_state_ref[...] = state
    entity_ref[...] = et_ref[...] - LEARN_RATE * grad / jnp.sqrt(state)


def call(kernel, outs, *args, scratch=(), flops=0):
    shapes = [jax.ShapeDtypeStruct(shape, F32) for shape in outs]
    moved = sum(4 * a.size for a in args) + sum(4 * s.size for s in shapes)
    return pl.pallas_call(
        kernel,
        out_shape=shapes,
        scratch_shapes=list(scratch),
        cost_estimate=pl.CostEstimate(flops=flops, bytes_accessed=moved, transcendentals=0),
        compiler_params=pltpu.CompilerParams(vmem_limit_bytes=48 << 20),
    )(*args)


def per_device(entity, adagrad_state, relation, src_rows, dst_rows, rel_ids, bucket_counts, noise_rows):
    nz, ny, reps = lax.axis_size("z"), lax.axis_size("y"), lax.axis_size("rep")
    rows, features = entity.shape
    slots = src_rows.shape[3]
    parts = nz * ny
    edges = parts * slots
    fs = round_up(features, reps * 8) // reps
    width = round_up(features + 2, 128)

    def ordered(ids):
        return ids.reshape(nz, ny, slots).transpose(1, 0, 2)

    et = entity.T
    padded = jnp.pad(et, ((0, reps * fs - features), (0, 0)))
    mine = lax.dynamic_slice_in_dim(padded, lax.axis_index("rep") * fs, fs, 0)
    table = lax.all_gather(mine, "z")

    src = ordered(src_rows).reshape(1, edges)
    rel = ordered(rel_ids).reshape(1, edges)
    dst = ordered(dst_rows)
    noise = ordered(noise_rows)
    live = (jnp.arange(slots, dtype=jnp.int32) < bucket_counts.reshape(nz, ny).T[:, :, None]).astype(F32)
    live = live.reshape(1, edges)

    wanted = jnp.stack([noise.reshape(ny, -1), dst.reshape(ny, -1)], axis=1)
    wanted = jnp.broadcast_to(wanted[:, None], (ny, reps) + wanted.shape[1:])
    asked = lax.all_to_all(
        wanted.reshape(ny * reps, 2, nz * slots), ("y", "rep"), split_axis=0, concat_axis=0, tiled=True
    )
    asked = asked.reshape(ny * reps, 2, nz, slots).transpose(2, 1, 0, 3).reshape(nz, 1, -1)

    dst = dst.reshape(1, edges)
    noise = noise.reshape(1, edges)
    relt = jnp.pad(relation.T, ((0, 0), (0, round_up(relation.shape[0], 128) - relation.shape[0])))
    dense = (features, rows)
    unit = 2 * edges * features * rows
    qt, relation_rows, queries = call(
        functools.partial(query_kernel, nz, ny),
        [(features, edges), (features, edges), (parts, slots, width)],
        et, relt, src, rel, dst, live,
        flops=5 * unit,
    )
    queries = lax.all_to_all(queries, ("z", "y"), split_axis=0, concat_axis=0, tiled=True)
    (found,) = call(
        table_kernel,
        [(ny * reps, fs, 2 * nz * slots)],
        table, asked,
        scratch=[pltpu.VMEM((nz, fs, 2 * ny * reps * slots), F32)],
        flops=1000 * unit,
    )
    queries, found = lax.optimization_barrier((queries, found))
    (owned,) = call(owner_kernel, [dense], queries, et, flops=5 * unit)
    got = lax.all_to_all(found, ("y", "rep"), split_axis=0, concat_axis=0, tiled=True)
    coef, noise_grads = call(
        functools.partial(noise_kernel, nz, ny),
        [(edges, edges), (parts, slots, width)],
        got, qt, live, noise,
        flops=6 * unit,
    )
    noise_grads = lax.all_to_all(noise_grads, ("z", "y"), split_axis=0, concat_axis=0, tiled=True)
    (early,) = call(
        functools.partial(source_kernel, ny),
        [dense],
        got, qt, relation_rows, live, src, coef, owned,
        flops=5 * unit,
    )
    (partial,) = call(scatter_kernel, [(reps, fs, rows)], noise_grads, early, flops=2 * unit)
    shares = lax.all_to_all(partial, "rep", split_axis=0, concat_axis=0, tiled=True)
    summed = lax.all_gather(jnp.sum(shares, axis=0), "rep")
    new_entity, new_state = call(
        update_kernel, [dense, (1, rows)], summed, et, adagrad_state.reshape(1, rows)
    )
    return new_entity.T, new_state.reshape(rows)


def solution(mesh):
    dom, reps = mesh.devices.shape
    ny = 4 if dom >= 16 else 2
    split_mesh = Mesh(mesh.devices.reshape(dom // ny, ny, reps), ("z", "y", "rep"))
    zy = ("z", "y")
    return jax.shard_map(
        per_device,
        mesh=split_mesh,
        in_specs=(
            P(zy, None),
            P(zy),
            P(),
            P(zy, "rep", None, None),
            P(zy, "rep", None, None),
            P(zy, "rep", None, None),
            P(zy, "rep", None),
            P(zy, "rep", None),
        ),
        out_specs=(P(zy, None), P(zy)),
        check_vma=False,
    )
```

```python
import functools

import jax
import jax.numpy as jnp
from jax import lax
from jax.experimental import pallas as pl
from jax.experimental.pallas import tpu as pltpu
from jax.sharding import Mesh
from jax.sharding import PartitionSpec as P

LEARN_RATE = 0.3
F32 = jnp.float32
BF16 = jnp.bfloat16
NN = (((1,), (0,)), ((), ()))
NT = (((1,), (1,)), ((), ()))


def round_up(value, unit):
    return -(-value // unit) * unit


def one_hot(row, rows):
    place = lax.broadcasted_iota(jnp.int32, (rows, row.shape[1]), 0)
    return (place == row).astype(F32).astype(BF16)


def split(x, terms):
    out = []
    for _ in range(terms):
        part = x.astype(BF16)
        out.append(part)
        x = x - part.astype(F32)
    return out


def mul(a, b, dims=NN):
    return lax.dot_general(a, b, dims, preferred_element_type=F32)


def pick(x, hot, dims=NN, terms=3):
    n = x.shape[0]
    parts = [part.astype(F32) for part in split(x, terms)]
    out = mul(jnp.concatenate(parts, axis=0).astype(BF16), hot, dims)
    return sum(out[i * n : (i + 1) * n] for i in range(terms - 1, -1, -1))


def product(a, b, dims=NN):
    a_high, a_low = split(a, 2)
    b_high, b_low = split(b, 2)
    return mul(a_low, b_high, dims) + mul(a_high, b_low, dims) + mul(a_high, b_high, dims)


def swap_blocks(v, slots, lane):
    n, span = len(v), v[0].shape[1]
    k = n // 2
    while k:
        low = (lane & k) == 0
        w = list(v)
        for i in range(n):
            if not i & k:
                a, b = v[i], v[i + k]
                w[i] = jnp.where(low, a, pltpu.roll(b, k * slots, 1))
                w[i + k] = jnp.where(low, pltpu.roll(a, span - k * slots, 1), b)
        v = w
        k //= 2
    return v


def query_kernel(et_ref, relt_ref, src_ref, rel_ref, query_ref, relation_ref):
    source = pick(et_ref[...], one_hot(src_ref[...], et_ref.shape[1]))
    relation = pick(relt_ref[...], one_hot(rel_ref[...], relt_ref.shape[1]))
    query_ref[...] = source * relation
    relation_ref[...] = relation


def table_kernel(table_ref, ids_ref, out_ref, got_ref):
    nh, fs, rows = table_ref.shape
    devices, _, span = out_ref.shape
    n = 2 * nh
    slots = span // n

    def fetch(h, carry):
        got_ref[h] = pick(table_ref[h], one_hot(ids_ref[h], rows))
        return carry

    lax.fori_loop(0, nh, fetch, 0, unroll=2)
    lane = lax.broadcasted_iota(jnp.int32, (8, span), 1) // slots

    def turn(f8, carry):
        at = pl.ds(pl.multiple_of(f8 * 8, 8), 8)
        for tile in range(devices // n):
            v = []
            for kind in range(2):
                start = (kind * devices + tile * n) * slots
                v += [got_ref[h, at, start : start + span] for h in range(nh)]
            v = swap_blocks(v, slots, lane)
            for i in range(n):
                out_ref[tile * n + i, at, :] = v[i]
        return carry

    lax.fori_loop(0, fs // 8, turn, 0)


def scatter_kernel(msg_ref, ids_ref, out_ref, got_ref):
    nh, fs, rows = out_ref.shape
    devices, _, span = msg_ref.shape
    n = 2 * nh
    slots = span // n
    lane = lax.broadcasted_iota(jnp.int32, (8, span), 1) // slots

    def turn(f8, carry):
        at = pl.ds(pl.multiple_of(f8 * 8, 8), 8)
        for tile in range(devices // n):
            v = swap_blocks([msg_ref[tile * n + i, at, :] for i in range(n)], slots, lane)
            for kind in range(2):
                start = (kind * devices + tile * n) * slots
                for h in range(nh):
                    got_ref[h, at, start : start + span] = v[kind * nh + h]
        return carry

    lax.fori_loop(0, fs // 8, turn, 0)

    def add(h, carry):
        out_ref[h] = pick(got_ref[h], one_hot(ids_ref[h], rows), NT, 2)
        return carry

    lax.fori_loop(0, nh, add, 0, unroll=2)


def received(got_ref, ny, features):
    devices, fs, span = got_ref.shape
    per = devices // (2 * ny)
    low = lax.broadcasted_iota(jnp.int32, (1, span), 1) < span // 2
    noise, target = [], []
    for y in range(ny):
        first, second = (
            got_ref[(l * ny + y) * per : (l * ny + y + 1) * per].reshape(per * fs, span)[:features] for l in range(2)
        )
        noise.append(jnp.where(low, first, pltpu.roll(second, span // 2, 1)))
        target.append(jnp.where(low, pltpu.roll(first, span // 2, 1), second))
    return jnp.concatenate(noise, axis=1), jnp.concatenate(target, axis=1)


def send(msg_ref, ny, noise, target):
    devices, fs, span = msg_ref.shape
    per = devices // (2 * ny)
    low = lax.broadcasted_iota(jnp.int32, (1, span), 1) < span // 2
    rest = jnp.zeros((per * fs - noise.shape[0], span), F32)
    for y in range(ny):
        a, b = noise[:, y * span : (y + 1) * span], target[:, y * span : (y + 1) * span]
        first = jnp.where(low, a, pltpu.roll(b, span // 2, 1))
        second = jnp.where(low, pltpu.roll(a, span // 2, 1), b)
        for l, block in enumerate((first, second)):
            full = jnp.concatenate([block, rest], axis=0) if rest.shape[0] else block
            msg_ref[(l * ny + y) * per : (l * ny + y + 1) * per] = full.reshape(per, fs, span)


def coefficients(query, noise, target, live):
    coef = jax.nn.sigmoid(product(noise.T, query)) * live
    positive = jnp.sum(query * target, axis=0, keepdims=True)
    return coef, -jax.nn.sigmoid(-positive) * live


def terms_kernel(ny, got_ref, query_ref, live_ref, msg_ref):
    query = query_ref[...]
    noise, target = received(got_ref, ny, query.shape[0])
    coef, pos_coef = coefficients(query, noise, target, live_ref[...])
    send(msg_ref, ny, product(query, coef, NT), pos_coef * query)


def source_kernel(ny, got_ref, query_ref, relation_ref, live_ref, src_ref, out_ref):
    reps, fs, rows = out_ref.shape
    query = query_ref[...]
    features = query.shape[0]
    noise, target = received(got_ref, ny, features)
    coef, pos_coef = coefficients(query, noise, target, live_ref[...])
    grad = relation_ref[...] * (pos_coef * target + product(noise, coef))
    grad = pick(grad, one_hot(src_ref[...], rows), NT, 2)
    rest = reps * fs - features
    if rest:
        grad = jnp.concatenate([grad, jnp.zeros((rest, rows), F32)], axis=0)
    out_ref[...] = grad.reshape(reps, fs, rows)


def update_kernel(grad_ref, et_ref, state_ref, entity_ref, new_state_ref):
    features, rows = et_ref.shape
    grad = grad_ref[...].reshape(-1, rows)[:features]
    state = state_ref[...] + jnp.sum(grad * grad, axis=0, keepdims=True) * (1.0 / features)
    new_state_ref[...] = state
    entity_ref[...] = et_ref[...] - LEARN_RATE * grad / jnp.sqrt(state)


def call(kernel, outs, *args, scratch=(), flops=0):
    shapes = [jax.ShapeDtypeStruct(shape, F32) for shape in outs]
    moved = sum(4 * a.size for a in args) + sum(4 * s.size for s in shapes)
    return pl.pallas_call(
        kernel,
        out_shape=shapes,
        scratch_shapes=list(scratch),
        cost_estimate=pl.CostEstimate(flops=flops, bytes_accessed=moved, transcendentals=0),
        compiler_params=pltpu.CompilerParams(vmem_limit_bytes=48 << 20),
    )(*args)


def per_device(entity, adagrad_state, relation, src_rows, dst_rows, rel_ids, bucket_counts, noise_rows):
    nh, nl, ny, reps = (lax.axis_size(name) for name in ("h", "l", "y", "rep"))
    near = ("l", "y", "rep")
    devices = nl * ny * reps
    rows, features = entity.shape
    slots = src_rows.shape[3]
    edges = nh * nl * ny * slots
    fs = round_up(features, reps * 8) // reps

    def ordered(ids):
        return ids.reshape(nh, nl, ny, slots).transpose(2, 1, 0, 3).reshape(1, edges)

    et = entity.T
    padded = jnp.pad(et, ((0, reps * fs - features), (0, 0)))
    mine = lax.dynamic_slice_in_dim(padded, lax.axis_index("rep") * fs, fs, 0)
    table = lax.all_gather(mine, "h")

    wanted = jnp.stack([noise_rows.reshape(nh, nl, ny, slots), dst_rows.reshape(nh, nl, ny, slots)])
    wanted = wanted.transpose(2, 3, 0, 1, 4).reshape(nl, ny, 1, 2 * nh * slots)
    wanted = jnp.broadcast_to(wanted, (nl, ny, reps, 2 * nh * slots)).reshape(devices, -1)
    asked = lax.all_to_all(wanted, near, split_axis=0, concat_axis=0, tiled=True)
    asked = asked.reshape(devices, 2, nh, slots).transpose(2, 1, 0, 3).reshape(nh, 1, -1)

    src = ordered(src_rows)
    rel = ordered(rel_ids)
    live = jnp.arange(slots, dtype=jnp.int32) < bucket_counts.reshape(nh, nl, ny).transpose(2, 1, 0)[..., None]
    live = live.astype(F32).reshape(1, edges)
    relt = jnp.pad(relation.T, ((0, 0), (0, round_up(relation.shape[0], 128) - relation.shape[0])))

    unit = 2 * edges * features * rows
    message = (devices, fs, 2 * nh * slots)
    got_shape = pltpu.VMEM((nh, fs, 2 * devices * slots), F32)
    query, relation_rows = call(query_kernel, [(features, edges)] * 2, et, relt, src, rel, flops=5 * unit)
    (found,) = call(table_kernel, [message], table, asked, scratch=[got_shape], flops=8 * unit)
    got = lax.all_to_all(found, near, split_axis=0, concat_axis=0, tiled=True)
    (terms,) = call(functools.partial(terms_kernel, ny), [message], got, query, live, flops=6 * unit)
    terms = lax.all_to_all(terms, near, split_axis=0, concat_axis=0, tiled=True)
    (source,) = call(
        functools.partial(source_kernel, ny), [(reps, fs, rows)], got, query, relation_rows, live, src, flops=8 * unit
    )
    (partial,) = call(scatter_kernel, [(nh, fs, rows)], terms, asked, scratch=[got_shape], flops=8 * unit)
    grad = lax.psum_scatter(partial, "h", scatter_dimension=0)
    shares = lax.all_to_all(source, "rep", split_axis=0, concat_axis=0, tiled=True)
    summed = lax.all_gather(grad + jnp.sum(shares, axis=0), "rep")
    new_entity, new_state = call(
        update_kernel, [(features, rows), (1, rows)], summed, et, adagrad_state.reshape(1, rows)
    )
    return new_entity.T, new_state.reshape(rows)


def solution(mesh):
    dom, reps = mesh.devices.shape
    ny = 4 if dom >= 16 else 2
    axes = ("h", "l", "y", "rep")
    cut = Mesh(mesh.devices.reshape(dom // (2 * ny), 2, ny, reps), axes)
    part = axes[:3]
    return jax.shard_map(
        per_device,
        mesh=cut,
        in_specs=(
            P(part, None),
            P(part),
            P(),
            P(part, "rep", None, None),
            P(part, "rep", None, None),
            P(part, "rep", None, None),
            P(part, "rep", None),
            P(part, "rep", None),
        ),
        out_specs=(P(part, None), P(part)),
        check_vma=False,
    )
```

```python
import functools

import jax
import jax.numpy as jnp
from jax import lax
from jax.experimental import pallas as pl
from jax.experimental.pallas import tpu as pltpu
from jax.sharding import Mesh
from jax.sharding import PartitionSpec as P

LEARN_RATE = 0.3
F32 = jnp.float32
BF16 = jnp.bfloat16
NN = (((1,), (0,)), ((), ()))
NT = (((1,), (1,)), ((), ()))


def round_up(value, unit):
    return -(-value // unit) * unit


def one_hot(row, rows):
    place = lax.broadcasted_iota(jnp.int32, (rows, row.shape[1]), 0)
    return (place == row).astype(F32).astype(BF16)


def split(x, terms):
    out = []
    for _ in range(terms):
        part = x.astype(BF16)
        out.append(part)
        x = x - part.astype(F32)
    return out


def mul(a, b, dims=NN):
    return lax.dot_general(a, b, dims, preferred_element_type=F32)


def pick(x, hot, dims=NN, terms=3):
    n = x.shape[0]
    parts = [part.astype(F32) for part in split(x, terms)]
    out = mul(jnp.concatenate(parts, axis=0).astype(BF16), hot, dims)
    return sum(out[i * n : (i + 1) * n] for i in range(terms - 1, -1, -1))


def product(a, b, dims=NN):
    a_high, a_low = split(a, 2)
    b_high, b_low = split(b, 2)
    return mul(a_low, b_high, dims) + mul(a_high, b_low, dims) + mul(a_high, b_high, dims)


def swap_blocks(v, slots, lane):
    n, span = len(v), v[0].shape[1]
    k = n // 2
    while k:
        low = (lane & k) == 0
        w = list(v)
        for i in range(n):
            if not i & k:
                a, b = v[i], v[i + k]
                w[i] = jnp.where(low, a, pltpu.roll(b, k * slots, 1))
                w[i + k] = jnp.where(low, pltpu.roll(a, span - k * slots, 1), b)
        v = w
        k //= 2
    return v


def query_kernel(et_ref, relt_ref, src_ref, rel_ref, query_ref, relation_ref):
    source = pick(et_ref[...], one_hot(src_ref[...], et_ref.shape[1]))
    relation = pick(relt_ref[...], one_hot(rel_ref[...], relt_ref.shape[1]))
    query_ref[...] = source * relation
    relation_ref[...] = relation


def table_kernel(table_ref, ids_ref, out_ref, got_ref):
    nh, fs, rows = table_ref.shape
    devices, _, span = out_ref.shape
    n = 2 * nh
    slots = span // n

    def fetch(h, carry):
        got_ref[h] = pick(table_ref[h], one_hot(ids_ref[h], rows))
        return carry

    lax.fori_loop(0, nh, fetch, 0, unroll=2)
    lane = lax.broadcasted_iota(jnp.int32, (8, span), 1) // slots

    def turn(f8, carry):
        at = pl.ds(pl.multiple_of(f8 * 8, 8), 8)
        for tile in range(devices // n):
            v = []
            for kind in range(2):
                start = (kind * devices + tile * n) * slots
                v += [got_ref[h, at, start : start + span] for h in range(nh)]
            v = swap_blocks(v, slots, lane)
            for i in range(n):
                out_ref[tile * n + i, at, :] = v[i]
        return carry

    lax.fori_loop(0, fs // 8, turn, 0)


def scatter_kernel(msg_ref, ids_ref, first_ref, second_ref, got_ref):
    nh, cut, rows = first_ref.shape
    devices, fs, span = msg_ref.shape
    n = 2 * nh
    slots = span // n
    lane = lax.broadcasted_iota(jnp.int32, (8, span), 1) // slots

    def turn(f8, carry):
        at = pl.ds(pl.multiple_of(f8 * 8, 8), 8)
        for tile in range(devices // n):
            v = swap_blocks([msg_ref[tile * n + i, at, :] for i in range(n)], slots, lane)
            for kind in range(2):
                start = (kind * devices + tile * n) * slots
                for h in range(nh):
                    got_ref[h, at, start : start + span] = v[kind * nh + h]
        return carry

    lax.fori_loop(0, fs // 8, turn, 0)

    def add(h, carry):
        grad = pick(got_ref[h], one_hot(ids_ref[h], rows), NT, 2)
        first_ref[h] = grad[:cut]
        second_ref[h] = grad[cut:]
        return carry

    lax.fori_loop(0, nh, add, 0, unroll=2)


def received(got_ref, ny, features):
    devices, fs, span = got_ref.shape
    per = devices // (2 * ny)
    low = lax.broadcasted_iota(jnp.int32, (1, span), 1) < span // 2
    noise, target = [], []
    for y in range(ny):
        first, second = (
            got_ref[(l * ny + y) * per : (l * ny + y + 1) * per].reshape(per * fs, span)[:features] for l in range(2)
        )
        noise.append(jnp.where(low, first, pltpu.roll(second, span // 2, 1)))
        target.append(jnp.where(low, pltpu.roll(first, span // 2, 1), second))
    return jnp.concatenate(noise, axis=1), jnp.concatenate(target, axis=1)


def send(msg_ref, ny, noise, target):
    devices, fs, span = msg_ref.shape
    per = devices // (2 * ny)
    low = lax.broadcasted_iota(jnp.int32, (1, span), 1) < span // 2
    rest = jnp.zeros((per * fs - noise.shape[0], span), F32)
    for y in range(ny):
        a, b = noise[:, y * span : (y + 1) * span], target[:, y * span : (y + 1) * span]
        first = jnp.where(low, a, pltpu.roll(b, span // 2, 1))
        second = jnp.where(low, pltpu.roll(a, span // 2, 1), b)
        for l, block in enumerate((first, second)):
            full = jnp.concatenate([block, rest], axis=0) if rest.shape[0] else block
            msg_ref[(l * ny + y) * per : (l * ny + y + 1) * per] = full.reshape(per, fs, span)


def coefficients(query, noise, target, live):
    coef = jax.nn.sigmoid(product(noise.T, query)) * live
    positive = jnp.sum(query * target, axis=0, keepdims=True)
    return coef, -jax.nn.sigmoid(-positive) * live


def terms_kernel(ny, got_ref, query_ref, live_ref, msg_ref):
    query = query_ref[...]
    noise, target = received(got_ref, ny, query.shape[0])
    coef, pos_coef = coefficients(query, noise, target, live_ref[...])
    send(msg_ref, ny, product(query, coef, NT), pos_coef * query)


def source_kernel(ny, got_ref, query_ref, relation_ref, live_ref, src_ref, out_ref):
    reps, fs, rows = out_ref.shape
    query = query_ref[...]
    features = query.shape[0]
    noise, target = received(got_ref, ny, features)
    coef, pos_coef = coefficients(query, noise, target, live_ref[...])
    grad = relation_ref[...] * (pos_coef * target + product(noise, coef))
    grad = pick(grad, one_hot(src_ref[...], rows), NT, 2)
    rest = reps * fs - features
    if rest:
        grad = jnp.concatenate([grad, jnp.zeros((rest, rows), F32)], axis=0)
    out_ref[...] = grad.reshape(reps, fs, rows)


def update_kernel(grad_ref, et_ref, state_ref, entity_ref, new_state_ref):
    features, rows = et_ref.shape
    grad = grad_ref[...].reshape(-1, rows)[:features]
    state = state_ref[...] + jnp.sum(grad * grad, axis=0, keepdims=True) * (1.0 / features)
    new_state_ref[...] = state
    entity_ref[...] = et_ref[...] - LEARN_RATE * grad / jnp.sqrt(state)


def call(kernel, outs, *args, scratch=(), flops=0):
    shapes = [jax.ShapeDtypeStruct(shape, F32) for shape in outs]
    moved = sum(4 * a.size for a in args) + sum(4 * s.size for s in shapes)
    return pl.pallas_call(
        kernel,
        out_shape=shapes,
        scratch_shapes=list(scratch),
        cost_estimate=pl.CostEstimate(flops=flops, bytes_accessed=moved, transcendentals=0),
        compiler_params=pltpu.CompilerParams(vmem_limit_bytes=48 << 20),
    )(*args)


def per_device(entity, adagrad_state, relation, src_rows, dst_rows, rel_ids, bucket_counts, noise_rows):
    nh, nl, ny, reps = (lax.axis_size(name) for name in ("h", "l", "y", "rep"))
    near = ("l", "y", "rep")
    devices = nl * ny * reps
    rows, features = entity.shape
    slots = src_rows.shape[3]
    edges = nh * nl * ny * slots
    fs = round_up(features, reps * 8) // reps

    def ordered(ids):
        return ids.reshape(nh, nl, ny, slots).transpose(2, 1, 0, 3).reshape(1, edges)

    et = entity.T
    padded = jnp.pad(et, ((0, reps * fs - features), (0, 0)))
    mine = lax.dynamic_slice_in_dim(padded, lax.axis_index("rep") * fs, fs, 0)
    table = lax.all_gather(mine, "h")

    wanted = jnp.stack([noise_rows.reshape(nh, nl, ny, slots), dst_rows.reshape(nh, nl, ny, slots)])
    wanted = wanted.transpose(2, 3, 0, 1, 4).reshape(nl, ny, 1, 2 * nh * slots)
    wanted = jnp.broadcast_to(wanted, (nl, ny, reps, 2 * nh * slots)).reshape(devices, -1)
    asked = lax.all_to_all(wanted, near, split_axis=0, concat_axis=0, tiled=True)
    asked = asked.reshape(devices, 2, nh, slots).transpose(2, 1, 0, 3).reshape(nh, 1, -1)

    src = ordered(src_rows)
    rel = ordered(rel_ids)
    live = jnp.arange(slots, dtype=jnp.int32) < bucket_counts.reshape(nh, nl, ny).transpose(2, 1, 0)[..., None]
    live = live.astype(F32).reshape(1, edges)
    relt = jnp.pad(relation.T, ((0, 0), (0, round_up(relation.shape[0], 128) - relation.shape[0])))

    unit = 2 * edges * features * rows
    message = (devices, fs, 2 * nh * slots)
    got_shape = pltpu.VMEM((nh, fs, 2 * devices * slots), F32)
    query, relation_rows = call(query_kernel, [(features, edges)] * 2, et, relt, src, rel, flops=5 * unit)
    (found,) = call(table_kernel, [message], table, asked, scratch=[got_shape], flops=8 * unit)
    got = lax.all_to_all(found, near, split_axis=0, concat_axis=0, tiled=True)
    (terms,) = call(functools.partial(terms_kernel, ny), [message], got, query, live, flops=6 * unit)
    terms = lax.all_to_all(terms, near, split_axis=0, concat_axis=0, tiled=True)
    (source,) = call(
        functools.partial(source_kernel, ny), [(reps, fs, rows)], got, query, relation_rows, live, src, flops=8 * unit
    )
    source = lax.psum_scatter(source, "rep", scatter_dimension=0)
    cut = round_up(3 * fs // 8, 8)
    first, second = call(
        scatter_kernel, [(nh, cut, rows), (nh, fs - cut, rows)], terms, asked, scratch=[got_shape], flops=8 * unit
    )
    second = lax.psum_scatter(second, "h", scatter_dimension=0)
    first = jnp.sum(lax.all_to_all(first, "h", split_axis=0, concat_axis=0, tiled=True), axis=0)
    summed = lax.all_gather(source + jnp.concatenate([first, second], axis=0), "rep")
    new_entity, new_state = call(
        update_kernel, [(features, rows), (1, rows)], summed, et, adagrad_state.reshape(1, rows)
    )
    return new_entity.T, new_state.reshape(rows)


def solution(mesh):
    dom, reps = mesh.devices.shape
    ny = 4 if dom >= 16 else 2
    axes = ("h", "l", "y", "rep")
    cut = Mesh(mesh.devices.reshape(dom // (2 * ny), 2, ny, reps), axes)
    part = axes[:3]
    return jax.shard_map(
        per_device,
        mesh=cut,
        in_specs=(
            P(part, None),
            P(part),
            P(),
            P(part, "rep", None, None),
            P(part, "rep", None, None),
            P(part, "rep", None, None),
            P(part, "rep", None),
            P(part, "rep", None),
        ),
        out_specs=(P(part, None), P(part)),
        check_vma=False,
    )
```

```python
import functools
import math

import jax
import jax.numpy as jnp
from jax import lax
from jax.experimental import pallas as pl
from jax.experimental.pallas import tpu as pltpu
from jax.sharding import Mesh
from jax.sharding import PartitionSpec as P

LEARN_RATE = 0.3
F32 = jnp.float32
BF16 = jnp.bfloat16
NN = (((1,), (0,)), ((), ()))
NT = (((1,), (1,)), ((), ()))


def round_up(value, unit):
    return -(-value // unit) * unit


def one_hot(row, rows):
    place = lax.broadcasted_iota(jnp.int32, (rows, row.shape[1]), 0)
    return (place == row).astype(F32).astype(BF16)


def split(x, terms):
    out = []
    for _ in range(terms):
        part = x.astype(BF16)
        out.append(part)
        x = x - part.astype(F32)
    return out


def mul(a, b, dims=NN):
    return lax.dot_general(a, b, dims, preferred_element_type=F32)


def pick(x, hot, dims=NN, terms=3):
    n = x.shape[0]
    parts = [part.astype(F32) for part in split(x, terms)]
    out = mul(jnp.concatenate(parts, axis=0).astype(BF16), hot, dims)
    return sum(out[i * n : (i + 1) * n] for i in range(terms - 1, -1, -1))


def product(a, b, dims=NN):
    a_high, a_low = split(a, 2)
    b_high, b_low = split(b, 2)
    return mul(a_low, b_high, dims) + mul(a_high, b_low, dims) + mul(a_high, b_high, dims)


def swap_blocks(v, slots, lane):
    n, span = len(v), v[0].shape[1]
    k = n // 2
    while k:
        low = (lane & k) == 0
        w = list(v)
        for i in range(n):
            if not i & k:
                a, b = v[i], v[i + k]
                w[i] = jnp.where(low, a, pltpu.roll(b, k * slots, 1))
                w[i + k] = jnp.where(low, pltpu.roll(a, span - k * slots, 1), b)
        v = w
        k //= 2
    return v


def order_kernel(nh, nl, ny, *refs):
    given, (src_out, rel_out, live_out, wanted_ref), held, sems = refs[:5], refs[5:9], refs[9:14], refs[14]
    copies = [pltpu.make_async_copy(a, b, sems.at[i]) for i, (a, b) in enumerate(zip(given, held))]
    for copy in copies:
        copy.start()
    for copy in copies:
        copy.wait()
    src_ref, rel_ref, dst_ref, noise_ref, count_ref = held
    slots, parts = src_ref.shape
    edges = parts * slots
    lane = lax.broadcasted_iota(jnp.int32, (1, edges), 1)
    slot, group = lane % slots, lane // slots
    h, l, y = group % nh, group // nh % nl, group // (nh * nl)
    part = (h * nl + l) * ny + y
    here = one_hot(part, parts)
    stack = jnp.concatenate([src_ref[...], rel_ref[...], dst_ref[...]], axis=0).astype(F32)
    spread = pick(stack, here, terms=2)
    row = lax.broadcasted_iota(jnp.int32, (slots, edges), 0)

    def own(i):
        mine = jnp.where(row == slot, spread[i * slots : (i + 1) * slots], 0.0)
        return jnp.sum(mine, axis=0, keepdims=True).astype(jnp.int32)

    src_out[...] = own(0)
    rel_out[...] = own(1)
    target = own(2)
    wide = jnp.broadcast_to(noise_ref[...].astype(F32), (8, edges))
    noise = pick(wide, one_hot(part * slots + slot, edges), terms=2)[:1].astype(jnp.int32)
    wide = jnp.broadcast_to(count_ref[...].astype(F32), (8, parts))
    count = mul(wide.astype(BF16), here)[:1].astype(jnp.int32)
    live_out[...] = (slot < count).astype(F32)
    devices, span = wanted_ref.shape
    per = devices // (nl * ny)
    low = lax.broadcasted_iota(jnp.int32, (1, span), 1) < span // 2
    for i in range(ny):
        a, b = noise[:, i * span : (i + 1) * span], target[:, i * span : (i + 1) * span]
        first = jnp.where(low, a, pltpu.roll(b, span // 2, 1))
        second = jnp.where(low, pltpu.roll(a, span // 2, 1), b)
        for k, block in enumerate((first, second)):
            wanted_ref[(k * ny + i) * per : (k * ny + i + 1) * per] = jnp.broadcast_to(block, (per, span))


def queries(et_ref, relt_ref, src_ref, rel_ref):
    source = pick(et_ref[...], one_hot(src_ref[...], et_ref.shape[1]))
    relation = pick(relt_ref[...], one_hot(rel_ref[...], relt_ref.shape[1]))
    return source * relation, relation


def table_kernel(table_ref, ids_ref, out_ref, got_ref):
    nh, fs, rows = table_ref.shape
    devices, _, span = out_ref.shape
    n = 2 * nh
    slots = span // n

    def fetch(h, carry):
        got_ref[h] = pick(table_ref[h], one_hot(ids_ref[h], rows))
        return carry

    lax.fori_loop(0, nh, fetch, 0, unroll=2)
    lane = lax.broadcasted_iota(jnp.int32, (8, span), 1) // slots

    def turn(f8, carry):
        at = pl.ds(pl.multiple_of(f8 * 8, 8), 8)
        for tile in range(devices // n):
            v = []
            for kind in range(2):
                start = (kind * devices + tile * n) * slots
                v += [got_ref[h, at, start : start + span] for h in range(nh)]
            v = swap_blocks(v, slots, lane)
            for i in range(n):
                out_ref[tile * n + i, at, :] = v[i]
        return carry

    lax.fori_loop(0, fs // 8, turn, 0)


def scatter_kernel(msg_ref, ids_ref, out_ref, got_ref, sum_ref, sems):
    nh, fs, rows = out_ref.shape
    devices, _, span = msg_ref.shape
    n = 2 * nh
    slots = span // n
    lane = lax.broadcasted_iota(jnp.int32, (8, span), 1) // slots

    def turn(f8, carry):
        at = pl.ds(pl.multiple_of(f8 * 8, 8), 8)
        for tile in range(devices // n):
            v = swap_blocks([msg_ref[tile * n + i, at, :] for i in range(n)], slots, lane)
            for kind in range(2):
                start = (kind * devices + tile * n) * slots
                for h in range(nh):
                    got_ref[h, at, start : start + span] = v[kind * nh + h]
        return carry

    lax.fori_loop(0, fs // 8, turn, 0)

    copies = []
    for h in range(nh):
        sum_ref[h] = pick(got_ref[h], one_hot(ids_ref[h], rows), NT, 2)
        copies.append(pltpu.make_async_copy(sum_ref.at[h], out_ref.at[h], sems.at[h]))
        copies[-1].start()
    for copy in copies:
        copy.wait()


def received(got_ref, ny, features):
    devices, fs, span = got_ref.shape
    per = devices // (2 * ny)
    low = lax.broadcasted_iota(jnp.int32, (1, span), 1) < span // 2
    noise, target = [], []
    for y in range(ny):
        first, second = (
            got_ref[(l * ny + y) * per : (l * ny + y + 1) * per].reshape(per * fs, span)[:features] for l in range(2)
        )
        noise.append(jnp.where(low, first, pltpu.roll(second, span // 2, 1)))
        target.append(jnp.where(low, pltpu.roll(first, span // 2, 1), second))
    return jnp.concatenate(noise, axis=1), jnp.concatenate(target, axis=1)


def send(msg_ref, ny, noise, target):
    devices, fs, span = msg_ref.shape
    per = devices // (2 * ny)
    low = lax.broadcasted_iota(jnp.int32, (1, span), 1) < span // 2
    rest = jnp.zeros((per * fs - noise.shape[0], span), F32)
    for y in range(ny):
        a, b = noise[:, y * span : (y + 1) * span], target[:, y * span : (y + 1) * span]
        first = jnp.where(low, a, pltpu.roll(b, span // 2, 1))
        second = jnp.where(low, pltpu.roll(a, span // 2, 1), b)
        for l, block in enumerate((first, second)):
            full = jnp.concatenate([block, rest], axis=0) if rest.shape[0] else block
            msg_ref[(l * ny + y) * per : (l * ny + y + 1) * per] = full.reshape(per, fs, span)


def coefficients(query, noise, target, live):
    coef = jax.nn.sigmoid(product(noise.T, query)) * live
    positive = jnp.sum(query * target, axis=0, keepdims=True)
    return coef, -jax.nn.sigmoid(-positive) * live


def terms_kernel(ny, got_ref, et_ref, relt_ref, src_ref, rel_ref, live_ref, msg_ref):
    query, _ = queries(et_ref, relt_ref, src_ref, rel_ref)
    noise, target = received(got_ref, ny, query.shape[0])
    coef, pos_coef = coefficients(query, noise, target, live_ref[...])
    send(msg_ref, ny, product(query, coef, NT), pos_coef * query)


def source_kernel(ny, got_ref, et_ref, relt_ref, src_ref, rel_ref, live_ref, out_ref):
    reps, fs, rows = out_ref.shape
    query, relation = queries(et_ref, relt_ref, src_ref, rel_ref)
    features = query.shape[0]
    noise, target = received(got_ref, ny, features)
    coef, pos_coef = coefficients(query, noise, target, live_ref[...])
    grad = relation * (pos_coef * target + product(noise, coef))
    grad = pick(grad, one_hot(src_ref[...], rows), NT, 2)
    rest = reps * fs - features
    if rest:
        grad = jnp.concatenate([grad, jnp.zeros((rest, rows), F32)], axis=0)
    out_ref[...] = grad.reshape(reps, fs, rows)


def update_kernel(grad_ref, et_ref, state_ref, entity_ref, new_state_ref):
    features, rows = et_ref.shape
    grad = grad_ref[...].reshape(-1, rows)[:features]
    state = state_ref[...] + jnp.sum(grad * grad, axis=0, keepdims=True) * (1.0 / features)
    new_state_ref[...] = state
    entity_ref[...] = et_ref[...] - LEARN_RATE * grad / jnp.sqrt(state)


def floats(*shapes):
    return [(shape, F32) for shape in shapes]


def call(kernel, outs, *args, scratch=(), flops=0, inputs=pltpu.VMEM, outputs=pltpu.VMEM):
    make = pltpu.HBM if outputs == pltpu.HBM else jax.ShapeDtypeStruct
    shapes = [make(shape, dtype) for shape, dtype in outs]
    moved = sum(4 * a.size for a in args) + sum(4 * math.prod(shape) for shape, _ in outs)
    return pl.pallas_call(
        kernel,
        out_shape=shapes,
        in_specs=[pl.BlockSpec(memory_space=inputs)] * len(args),
        out_specs=[pl.BlockSpec(memory_space=outputs)] * len(outs),
        scratch_shapes=list(scratch),
        cost_estimate=pl.CostEstimate(flops=flops, bytes_accessed=moved, transcendentals=0),
        compiler_params=pltpu.CompilerParams(vmem_limit_bytes=48 << 20),
    )(*args)


def per_device(entity, adagrad_state, relation, src_rows, dst_rows, rel_ids, bucket_counts, noise_rows):
    nh, nl, ny, reps = (lax.axis_size(name) for name in ("h", "l", "y", "rep"))
    near = ("l", "y", "rep")
    devices = nl * ny * reps
    rows, features = entity.shape
    slots = src_rows.shape[3]
    edges = nh * nl * ny * slots
    fs = round_up(features, reps * 8) // reps

    et = entity.T
    padded = jnp.pad(et, ((0, reps * fs - features), (0, 0)))
    mine = lax.dynamic_slice_in_dim(padded, lax.axis_index("rep") * fs, fs, 0)
    table = lax.all_gather(mine, "h")

    def turned(ids):
        return ids.reshape(nh * nl * ny, slots).T

    given = [turned(ids) for ids in (src_rows, rel_ids, dst_rows)]
    given += [noise_rows.reshape(1, edges), bucket_counts.reshape(1, -1)]
    row = ((1, edges), jnp.int32)
    src, rel, live, wanted = call(
        functools.partial(order_kernel, nh, nl, ny),
        [row, row, ((1, edges), F32), ((devices, 2 * nh * slots), jnp.int32)],
        *(pltpu.with_memory_space_constraint(a, pltpu.HBM) for a in given),
        scratch=[pltpu.VMEM(a.shape, a.dtype) for a in given] + [pltpu.SemaphoreType.DMA((len(given),))],
        inputs=pltpu.HBM,
    )
    asked = lax.all_to_all(wanted, near, split_axis=0, concat_axis=0, tiled=True)
    asked = asked.reshape(devices, 2, nh, slots).transpose(2, 1, 0, 3).reshape(nh, 1, -1)
    relt = relation.T

    unit = 2 * edges * features * rows
    message = (devices, fs, 2 * nh * slots)
    got_shape = pltpu.VMEM((nh, fs, 2 * devices * slots), F32)
    (found,) = call(table_kernel, floats(message), table, asked, scratch=[got_shape], flops=8 * unit)
    got = lax.all_to_all(found, near, split_axis=0, concat_axis=0, tiled=True)
    edge_args = (got, et, relt, src, rel, live)
    (terms,) = call(functools.partial(terms_kernel, ny), floats(message), *edge_args, flops=11 * unit)
    terms = lax.all_to_all(terms, near, split_axis=0, concat_axis=0, tiled=True)
    (partial,) = call(
        scatter_kernel,
        floats((nh, fs, rows)),
        terms, asked,
        scratch=[got_shape, pltpu.VMEM((nh, fs, rows), F32), pltpu.SemaphoreType.DMA((nh,))],
        flops=8 * unit,
        outputs=pltpu.HBM,
    )
    (source,) = call(functools.partial(source_kernel, ny), floats((reps, fs, rows)), *edge_args, flops=13 * unit)
    grad = lax.psum_scatter(partial, "h", scatter_dimension=0)
    shares = lax.all_to_all(source, "rep", split_axis=0, concat_axis=0, tiled=True)
    summed = lax.all_gather(grad + jnp.sum(shares, axis=0), "rep")
    new_entity, new_state = call(
        update_kernel, floats((features, rows), (1, rows)), summed, et, adagrad_state.reshape(1, rows)
    )
    return new_entity.T, new_state.reshape(rows)


def solution(mesh):
    dom, reps = mesh.devices.shape
    ny = 4 if dom >= 16 else 2
    axes = ("h", "l", "y", "rep")
    cut = Mesh(mesh.devices.reshape(dom // (2 * ny), 2, ny, reps), axes)
    part = axes[:3]
    return jax.shard_map(
        per_device,
        mesh=cut,
        in_specs=(
            P(part, None),
            P(part),
            P(),
            P(part, "rep", None, None),
            P(part, "rep", None, None),
            P(part, "rep", None, None),
            P(part, "rep", None),
            P(part, "rep", None),
        ),
        out_specs=(P(part, None), P(part)),
        check_vma=False,
    )
```

```python
import functools
import math

import jax
import jax.numpy as jnp
from jax import lax
from jax.experimental import pallas as pl
from jax.experimental.pallas import tpu as pltpu
from jax.sharding import Mesh
from jax.sharding import PartitionSpec as P

LEARN_RATE = 0.3
F32 = jnp.float32
BF16 = jnp.bfloat16
NN = (((1,), (0,)), ((), ()))
NT = (((1,), (1,)), ((), ()))


def round_up(value, unit):
    return -(-value // unit) * unit


def one_hot(row, rows):
    place = lax.broadcasted_iota(jnp.int32, (rows, row.shape[1]), 0)
    return (place == row).astype(F32).astype(BF16)


def split(x, terms):
    out = []
    for _ in range(terms):
        part = x.astype(BF16)
        out.append(part)
        x = x - part.astype(F32)
    return out


def mul(a, b, dims=NN):
    return lax.dot_general(a, b, dims, preferred_element_type=F32)


def pick(x, hot, dims=NN, terms=3):
    n = x.shape[0]
    parts = [part.astype(F32) for part in split(x, terms)]
    out = mul(jnp.concatenate(parts, axis=0).astype(BF16), hot, dims)
    return sum(out[i * n : (i + 1) * n] for i in range(terms - 1, -1, -1))


def product(a, b, dims=NN):
    a_high, a_low = split(a, 2)
    b_high, b_low = split(b, 2)
    return mul(a_low, b_high, dims) + mul(a_high, b_low, dims) + mul(a_high, b_high, dims)


def swap_blocks(v, slots, lane):
    n, span = len(v), v[0].shape[1]
    k = n // 2
    while k:
        low = (lane & k) == 0
        w = list(v)
        for i in range(n):
            if not i & k:
                a, b = v[i], v[i + k]
                w[i] = jnp.where(low, a, pltpu.roll(b, k * slots, 1))
                w[i + k] = jnp.where(low, pltpu.roll(a, span - k * slots, 1), b)
        v = w
        k //= 2
    return v


def order_kernel(nh, nl, ny, *refs):
    given, (src_out, rel_out, live_out, wanted_ref), held, sems = refs[:5], refs[5:9], refs[9:14], refs[14]
    copies = [pltpu.make_async_copy(a, b, sems.at[i]) for i, (a, b) in enumerate(zip(given, held))]
    for copy in copies:
        copy.start()
    for copy in copies:
        copy.wait()
    src_ref, rel_ref, dst_ref, noise_ref, count_ref = held
    slots, parts = src_ref.shape
    edges = parts * slots
    lane = lax.broadcasted_iota(jnp.int32, (1, edges), 1)
    slot, group = lane % slots, lane // slots
    h, l, y = group % nh, group // nh % nl, group // (nh * nl)
    part = (h * nl + l) * ny + y
    here = one_hot(part, parts)
    stack = jnp.concatenate([src_ref[...], rel_ref[...], dst_ref[...]], axis=0).astype(F32)
    spread = pick(stack, here, terms=2)
    row = lax.broadcasted_iota(jnp.int32, (slots, edges), 0)

    def own(i):
        mine = jnp.where(row == slot, spread[i * slots : (i + 1) * slots], 0.0)
        return jnp.sum(mine, axis=0, keepdims=True).astype(jnp.int32)

    src_out[...] = own(0)
    rel_out[...] = own(1)
    target = own(2)
    wide = jnp.broadcast_to(noise_ref[...].astype(F32), (8, edges))
    noise = pick(wide, one_hot(part * slots + slot, edges), terms=2)[:1].astype(jnp.int32)
    wide = jnp.broadcast_to(count_ref[...].astype(F32), (8, parts))
    count = mul(wide.astype(BF16), here)[:1].astype(jnp.int32)
    live_out[...] = (slot < count).astype(F32)
    devices, span = wanted_ref.shape
    per = devices // (nl * ny)
    low = lax.broadcasted_iota(jnp.int32, (1, span), 1) < span // 2
    for i in range(ny):
        a, b = noise[:, i * span : (i + 1) * span], target[:, i * span : (i + 1) * span]
        first = jnp.where(low, a, pltpu.roll(b, span // 2, 1))
        second = jnp.where(low, pltpu.roll(a, span // 2, 1), b)
        for k, block in enumerate((first, second)):
            wanted_ref[(k * ny + i) * per : (k * ny + i + 1) * per] = jnp.broadcast_to(block, (per, span))


def queries(et_ref, relt_ref, src_ref, rel_ref):
    source = pick(et_ref[...], one_hot(src_ref[...], et_ref.shape[1]))
    relation = pick(relt_ref[...], one_hot(rel_ref[...], relt_ref.shape[1]))
    return source * relation, relation


def chunks(fs):
    return list(range(0, fs - 7, 8)) + ([fs - 8] if fs % 8 else [])


def table_kernel(fs, table_ref, ids_ref, out_ref, got_ref, stack_ref):
    nh, held, lanes = got_ref.shape
    span = out_ref.shape[1]
    devices = out_ref.shape[0] // fs
    tiles = table_ref.shape[0] // (nh * fs)
    n = 2 * nh
    slots = span // n
    terms = stack_ref.shape[0] // held

    for h in range(nh):
        for t in range(tiles):
            rows = table_ref[pl.ds(h * tiles * fs + t, fs, stride=tiles), :]
            for i, part in enumerate(split(rows, terms)):
                stack_ref[i * held : i * held + fs, t * 128 : (t + 1) * 128] = part.astype(F32)
        found = mul(stack_ref[...].astype(BF16), one_hot(ids_ref[h], tiles * 128))
        got_ref[h] = sum(found[i * held : (i + 1) * held] for i in range(terms - 1, -1, -1))
    lane = lax.broadcasted_iota(jnp.int32, (8, span), 1) // slots

    def turn(tile, carry):
        for f in chunks(fs):
            v = []
            for kind in range(2):
                start = pl.multiple_of((kind * devices + tile * n) * slots, span)
                v += [got_ref[h, f : f + 8, pl.ds(start, span)] for h in range(nh)]
            v = swap_blocks(v, slots, lane)
            for i in range(n):
                out_ref[pl.ds((tile * n + i) * fs + f, 8), :] = v[i]
        return carry

    lax.fori_loop(0, devices // n, turn, 0)


def scatter_kernel(fs, msg_ref, ids_ref, out_ref, got_ref, sum_ref, sems):
    nh, held, lanes = got_ref.shape
    span = msg_ref.shape[1]
    devices = msg_ref.shape[0] // fs
    tiles = out_ref.shape[1] // fs
    n = 2 * nh
    slots = span // n
    lane = lax.broadcasted_iota(jnp.int32, (8, span), 1) // slots

    def turn(tile, carry):
        for f in chunks(fs):
            v = swap_blocks([msg_ref[pl.ds((tile * n + i) * fs + f, 8), :] for i in range(n)], slots, lane)
            for kind in range(2):
                start = pl.multiple_of((kind * devices + tile * n) * slots, span)
                for h in range(nh):
                    got_ref[h, f : f + 8, pl.ds(start, span)] = v[kind * nh + h]
        return carry

    lax.fori_loop(0, devices // n, turn, 0)

    copies = []
    for h in range(nh):
        grad = pick(got_ref[h], one_hot(ids_ref[h], tiles * 128), NT, 2)
        for t in range(tiles):
            sum_ref[h, t * fs : (t + 1) * fs] = grad[:fs, t * 128 : (t + 1) * 128]
        copies.append(pltpu.make_async_copy(sum_ref.at[h], out_ref.at[h], sems.at[h]))
        copies[-1].start()
    for copy in copies:
        copy.wait()


def received(got_ref, ny, features):
    span = got_ref.shape[1]
    low = lax.broadcasted_iota(jnp.int32, (1, span), 1) < span // 2
    noise, target = [], []
    for y in range(ny):
        first, second = (got_ref[(l * ny + y) * features : (l * ny + y + 1) * features] for l in range(2))
        noise.append(jnp.where(low, first, pltpu.roll(second, span // 2, 1)))
        target.append(jnp.where(low, pltpu.roll(first, span // 2, 1), second))
    return jnp.concatenate(noise, axis=1), jnp.concatenate(target, axis=1)


def send(msg_ref, ny, noise, target):
    features, span = noise.shape[0], msg_ref.shape[1]
    low = lax.broadcasted_iota(jnp.int32, (1, span), 1) < span // 2
    for y in range(ny):
        a, b = noise[:, y * span : (y + 1) * span], target[:, y * span : (y + 1) * span]
        first = jnp.where(low, a, pltpu.roll(b, span // 2, 1))
        second = jnp.where(low, pltpu.roll(a, span // 2, 1), b)
        for l, block in enumerate((first, second)):
            msg_ref[(l * ny + y) * features : (l * ny + y + 1) * features] = block


def coefficients(query, noise, target, live):
    coef = jax.nn.sigmoid(product(noise.T, query)) * live
    positive = jnp.sum(query * target, axis=0, keepdims=True)
    return coef, -jax.nn.sigmoid(-positive) * live


def terms_kernel(ny, got_ref, et_ref, relt_ref, src_ref, rel_ref, live_ref, msg_ref):
    query, _ = queries(et_ref, relt_ref, src_ref, rel_ref)
    noise, target = received(got_ref, ny, query.shape[0])
    coef, pos_coef = coefficients(query, noise, target, live_ref[...])
    send(msg_ref, ny, product(query, coef, NT), pos_coef * query)


def source_kernel(ny, reps, got_ref, et_ref, relt_ref, src_ref, rel_ref, live_ref, out_ref):
    query, relation = queries(et_ref, relt_ref, src_ref, rel_ref)
    features, rows = et_ref.shape
    fs, tiles = features // reps, rows // 128
    noise, target = received(got_ref, ny, features)
    coef, pos_coef = coefficients(query, noise, target, live_ref[...])
    grad = relation * (pos_coef * target + product(noise, coef))
    grad = pick(grad, one_hot(src_ref[...], rows), NT, 2)
    for r in range(reps):
        for t in range(tiles):
            at = (r * tiles + t) * fs
            out_ref[at : at + fs] = grad[r * fs : (r + 1) * fs, t * 128 : (t + 1) * 128]


def update_kernel(reps, grad_ref, et_ref, state_ref, entity_ref, new_state_ref):
    features, rows = et_ref.shape
    fs, tiles = features // reps, rows // 128
    for t in range(tiles):
        lanes = slice(t * 128, (t + 1) * 128)
        grads = [grad_ref[(r * tiles + t) * fs : (r * tiles + t + 1) * fs] for r in range(reps)]
        squares = sum(jnp.sum(grad * grad, axis=0, keepdims=True) for grad in grads)
        state = state_ref[:, lanes] + squares * (1.0 / features)
        new_state_ref[:, lanes] = state
        scale = LEARN_RATE / jnp.sqrt(state)
        for r, grad in enumerate(grads):
            at = slice(r * fs, (r + 1) * fs)
            entity_ref[at, lanes] = et_ref[at, lanes] - grad * scale


def floats(*shapes):
    return [(shape, F32) for shape in shapes]


def call(kernel, outs, *args, scratch=(), flops=0, inputs=pltpu.VMEM, outputs=pltpu.VMEM):
    make = pltpu.HBM if outputs == pltpu.HBM else jax.ShapeDtypeStruct
    shapes = [make(shape, dtype) for shape, dtype in outs]
    moved = sum(4 * a.size for a in args) + sum(4 * math.prod(shape) for shape, _ in outs)
    return pl.pallas_call(
        kernel,
        out_shape=shapes,
        in_specs=[pl.BlockSpec(memory_space=inputs)] * len(args),
        out_specs=[pl.BlockSpec(memory_space=outputs)] * len(outs),
        scratch_shapes=list(scratch),
        cost_estimate=pl.CostEstimate(flops=flops, bytes_accessed=moved, transcendentals=0),
        compiler_params=pltpu.CompilerParams(vmem_limit_bytes=48 << 20),
    )(*args)


def per_device(entity, adagrad_state, relation, src_rows, dst_rows, rel_ids, bucket_counts, noise_rows):
    nh, nl, ny, reps = (lax.axis_size(name) for name in ("h", "l", "y", "rep"))
    near = ("l", "y", "rep")
    devices = nl * ny * reps
    rows, features = entity.shape
    slots = src_rows.shape[3]
    edges = nh * nl * ny * slots
    fs, tiles = features // reps, rows // 128
    packed = tiles * fs

    et = entity.T
    mine = lax.dynamic_slice_in_dim(et, lax.axis_index("rep") * fs, fs, 0)
    table = lax.all_gather(mine.reshape(packed, 128), "h").reshape(nh * packed, 128)

    def turned(ids):
        return ids.reshape(nh * nl * ny, slots).T

    given = [turned(ids) for ids in (src_rows, rel_ids, dst_rows)]
    given += [noise_rows.reshape(1, edges), bucket_counts.reshape(1, -1)]
    row = ((1, edges), jnp.int32)
    src, rel, live, wanted = call(
        functools.partial(order_kernel, nh, nl, ny),
        [row, row, ((1, edges), F32), ((devices, 2 * nh * slots), jnp.int32)],
        *(pltpu.with_memory_space_constraint(a, pltpu.HBM) for a in given),
        scratch=[pltpu.VMEM(a.shape, a.dtype) for a in given] + [pltpu.SemaphoreType.DMA((len(given),))],
        inputs=pltpu.HBM,
    )
    asked = lax.all_to_all(wanted, near, split_axis=0, concat_axis=0, tiled=True)
    asked = asked.reshape(devices, 2, nh, slots).transpose(2, 1, 0, 3).reshape(nh, 1, -1)
    relt = relation.T

    unit = 2 * edges * features * rows
    span = 2 * nh * slots
    message = (devices * fs, span)
    wire = (devices, fs // 2, 2, span)
    held = round_up(fs, 8)
    got_shape = pltpu.VMEM((nh, held, 2 * devices * slots), F32)
    (found,) = call(
        functools.partial(table_kernel, fs),
        floats(message),
        table, asked,
        scratch=[got_shape, pltpu.VMEM((3 * held, rows), F32)],
        flops=8 * unit,
    )
    got = lax.all_to_all(found.reshape(wire), near, split_axis=0, concat_axis=0, tiled=True).reshape(message)
    edge_args = (got, et, relt, src, rel, live)
    (terms,) = call(functools.partial(terms_kernel, ny), floats(message), *edge_args, flops=11 * unit)
    terms = lax.all_to_all(terms.reshape(wire), near, split_axis=0, concat_axis=0, tiled=True).reshape(message)
    (partial,) = call(
        functools.partial(scatter_kernel, fs),
        floats((nh, packed, 128)),
        terms, asked,
        scratch=[got_shape, pltpu.VMEM((nh, packed, 128), F32), pltpu.SemaphoreType.DMA((nh,))],
        flops=8 * unit,
        outputs=pltpu.HBM,
    )
    (source,) = call(
        functools.partial(source_kernel, ny, reps), floats((reps * packed, 128)), *edge_args, flops=13 * unit
    )
    grad = lax.psum_scatter(partial, "h", scatter_dimension=0)
    shares = lax.all_to_all(source.reshape(reps, packed, 128), "rep", split_axis=0, concat_axis=0, tiled=True)
    summed = lax.all_gather(grad + jnp.sum(shares, axis=0), "rep").reshape(reps * packed, 128)
    new_entity, new_state = call(
        functools.partial(update_kernel, reps),
        floats((features, rows), (1, rows)),
        summed, et, adagrad_state.reshape(1, rows),
    )
    return new_entity.T, new_state.reshape(rows)


def solution(mesh):
    dom, reps = mesh.devices.shape
    ny = 4 if dom >= 16 else 2
    axes = ("h", "l", "y", "rep")
    cut = Mesh(mesh.devices.reshape(dom // (2 * ny), 2, ny, reps), axes)
    part = axes[:3]
    return jax.shard_map(
        per_device,
        mesh=cut,
        in_specs=(
            P(part, None),
            P(part),
            P(),
            P(part, "rep", None, None),
            P(part, "rep", None, None),
            P(part, "rep", None, None),
            P(part, "rep", None),
            P(part, "rep", None),
        ),
        out_specs=(P(part, None), P(part)),
        check_vma=False,
    )
```

```python
import functools
import math

import jax
import jax.numpy as jnp
from jax import lax
from jax.experimental import pallas as pl
from jax.experimental.pallas import tpu as pltpu
from jax.sharding import Mesh
from jax.sharding import PartitionSpec as P

LEARN_RATE = 0.3
F32 = jnp.float32
BF16 = jnp.bfloat16
NN = (((1,), (0,)), ((), ()))
NT = (((1,), (1,)), ((), ()))


def round_up(value, unit):
    return -(-value // unit) * unit


def one_hot(row, rows):
    place = lax.broadcasted_iota(jnp.int32, (rows, row.shape[1]), 0)
    return (place == row).astype(F32).astype(BF16)


def split(x, terms):
    out = []
    for _ in range(terms):
        part = x.astype(BF16)
        out.append(part)
        x = x - part.astype(F32)
    return out


def mul(a, b, dims=NN):
    return lax.dot_general(a, b, dims, preferred_element_type=F32)


def pick(x, hot, dims=NN, terms=3):
    n = x.shape[0]
    parts = [part.astype(F32) for part in split(x, terms)]
    out = mul(jnp.concatenate(parts, axis=0).astype(BF16), hot, dims)
    return sum(out[i * n : (i + 1) * n] for i in range(terms - 1, -1, -1))


def product(a, b, dims=NN):
    a_high, a_low = split(a, 2)
    b_high, b_low = split(b, 2)
    return mul(a_low, b_high, dims) + mul(a_high, b_low, dims) + mul(a_high, b_high, dims)


def swap_blocks(v, slots, lane):
    n, span = len(v), v[0].shape[1]
    k = n // 2
    while k:
        low = (lane & k) == 0
        w = list(v)
        for i in range(n):
            if not i & k:
                a, b = v[i], v[i + k]
                w[i] = jnp.where(low, a, pltpu.roll(b, k * slots, 1))
                w[i + k] = jnp.where(low, pltpu.roll(a, span - k * slots, 1), b)
        v = w
        k //= 2
    return v


def order_kernel(nh, nl, ny, *refs):
    given, (src_out, rel_out, live_out, wanted_ref), held, sems = refs[:5], refs[5:9], refs[9:14], refs[14]
    copies = [pltpu.make_async_copy(a, b, sems.at[i]) for i, (a, b) in enumerate(zip(given, held))]
    for copy in copies:
        copy.start()
    for copy in copies:
        copy.wait()
    src_ref, rel_ref, dst_ref, noise_ref, count_ref = held
    slots, parts = src_ref.shape
    edges = parts * slots
    lane = lax.broadcasted_iota(jnp.int32, (1, edges), 1)
    slot, group = lane % slots, lane // slots
    h, l, y = group % nh, group // nh % nl, group // (nh * nl)
    part = (h * nl + l) * ny + y
    here = one_hot(part, parts)
    stack = jnp.concatenate([src_ref[...], rel_ref[...], dst_ref[...]], axis=0).astype(F32)
    spread = pick(stack, here, terms=2)
    row = lax.broadcasted_iota(jnp.int32, (slots, edges), 0)

    def own(i):
        mine = jnp.where(row == slot, spread[i * slots : (i + 1) * slots], 0.0)
        return jnp.sum(mine, axis=0, keepdims=True).astype(jnp.int32)

    src_out[...] = own(0)
    rel_out[...] = own(1)
    target = own(2)
    wide = jnp.broadcast_to(noise_ref[...].astype(F32), (8, edges))
    noise = pick(wide, one_hot(part * slots + slot, edges), terms=2)[:1].astype(jnp.int32)
    wide = jnp.broadcast_to(count_ref[...].astype(F32), (8, parts))
    count = mul(wide.astype(BF16), here)[:1].astype(jnp.int32)
    live_out[...] = (slot < count).astype(F32)
    devices, span = wanted_ref.shape
    per = devices // (nl * ny)
    low = lax.broadcasted_iota(jnp.int32, (1, span), 1) < span // 2
    for i in range(ny):
        a, b = noise[:, i * span : (i + 1) * span], target[:, i * span : (i + 1) * span]
        first = jnp.where(low, a, pltpu.roll(b, span // 2, 1))
        second = jnp.where(low, pltpu.roll(a, span // 2, 1), b)
        for k, block in enumerate((first, second)):
            wanted_ref[(k * ny + i) * per : (k * ny + i + 1) * per] = jnp.broadcast_to(block, (per, span))


def queries(et_ref, relt_ref, src_ref, rel_ref):
    source = pick(et_ref[...], one_hot(src_ref[...], et_ref.shape[1]))
    relation = pick(relt_ref[...], one_hot(rel_ref[...], relt_ref.shape[1]))
    return source * relation, relation


def chunks(fs):
    return list(range(0, fs - 7, 8)) + ([fs - 8] if fs % 8 else [])


def table_kernel(fs, table_ref, ids_ref, out_ref, got_ref, stack_ref):
    nh, held, lanes = got_ref.shape
    span = out_ref.shape[1]
    devices = out_ref.shape[0] // fs
    tiles = table_ref.shape[0] // (nh * fs)
    n = 2 * nh
    slots = span // n
    terms = stack_ref.shape[0] // held

    for h in range(nh):
        for t in range(tiles):
            rows = table_ref[pl.ds(h * tiles * fs + t, fs, stride=tiles), :]
            for i, part in enumerate(split(rows, terms)):
                stack_ref[i * held : i * held + fs, t * 128 : (t + 1) * 128] = part.astype(F32)
        found = mul(stack_ref[...].astype(BF16), one_hot(ids_ref[h], tiles * 128))
        got_ref[h] = sum(found[i * held : (i + 1) * held] for i in range(terms - 1, -1, -1))
    lane = lax.broadcasted_iota(jnp.int32, (8, span), 1) // slots

    def turn(tile, carry):
        for f in chunks(fs):
            v = []
            for kind in range(2):
                start = pl.multiple_of((kind * devices + tile * n) * slots, span)
                v += [got_ref[h, f : f + 8, pl.ds(start, span)] for h in range(nh)]
            v = swap_blocks(v, slots, lane)
            for i in range(n):
                out_ref[pl.ds((tile * n + i) * fs + f, 8), :] = v[i]
        return carry

    lax.fori_loop(0, devices // n, turn, 0)


def scatter_kernel(fs, msg_ref, ids_ref, out_ref, got_ref, sum_ref, sems):
    nh, held, lanes = got_ref.shape
    span = msg_ref.shape[1]
    devices = msg_ref.shape[0] // fs
    tiles = out_ref.shape[1] // fs
    n = 2 * nh
    slots = span // n
    lane = lax.broadcasted_iota(jnp.int32, (8, span), 1) // slots

    def turn(tile, carry):
        for f in chunks(fs):
            v = swap_blocks([msg_ref[pl.ds((tile * n + i) * fs + f, 8), :] for i in range(n)], slots, lane)
            for kind in range(2):
                start = pl.multiple_of((kind * devices + tile * n) * slots, span)
                for h in range(nh):
                    got_ref[h, f : f + 8, pl.ds(start, span)] = v[kind * nh + h]
        return carry

    lax.fori_loop(0, devices // n, turn, 0)

    copies = []
    for h in range(nh):
        grad = pick(got_ref[h], one_hot(ids_ref[h], tiles * 128), NT, 2)
        for t in range(tiles):
            sum_ref[h, t * fs : (t + 1) * fs] = grad[:fs, t * 128 : (t + 1) * 128]
        copies.append(pltpu.make_async_copy(sum_ref.at[h], out_ref.at[h], sems.at[h]))
        copies[-1].start()
    for copy in copies:
        copy.wait()


def received(got_ref, ny, features):
    span = got_ref.shape[1]
    low = lax.broadcasted_iota(jnp.int32, (1, span), 1) < span // 2
    noise, target = [], []
    for y in range(ny):
        first, second = (got_ref[(l * ny + y) * features : (l * ny + y + 1) * features] for l in range(2))
        noise.append(jnp.where(low, first, pltpu.roll(second, span // 2, 1)))
        target.append(jnp.where(low, pltpu.roll(first, span // 2, 1), second))
    return jnp.concatenate(noise, axis=1), jnp.concatenate(target, axis=1)


def send(msg_ref, ny, noise, target):
    features, span = noise.shape[0], msg_ref.shape[1]
    low = lax.broadcasted_iota(jnp.int32, (1, span), 1) < span // 2
    for y in range(ny):
        a, b = noise[:, y * span : (y + 1) * span], target[:, y * span : (y + 1) * span]
        first = jnp.where(low, a, pltpu.roll(b, span // 2, 1))
        second = jnp.where(low, pltpu.roll(a, span // 2, 1), b)
        for l, block in enumerate((first, second)):
            msg_ref[(l * ny + y) * features : (l * ny + y + 1) * features] = block


def coefficients(query, noise, target, live):
    coef = jax.nn.sigmoid(product(noise.T, query)) * live
    positive = jnp.sum(query * target, axis=0, keepdims=True)
    return coef, -jax.nn.sigmoid(-positive) * live


def terms_kernel(ny, got_ref, et_ref, relt_ref, src_ref, rel_ref, live_ref, msg_ref):
    query, _ = queries(et_ref, relt_ref, src_ref, rel_ref)
    noise, target = received(got_ref, ny, query.shape[0])
    coef, pos_coef = coefficients(query, noise, target, live_ref[...])
    send(msg_ref, ny, product(query, coef, NT), pos_coef * query)


def source_kernel(ny, reps, got_ref, et_ref, relt_ref, src_ref, rel_ref, live_ref, out_ref):
    query, relation = queries(et_ref, relt_ref, src_ref, rel_ref)
    features, rows = et_ref.shape
    fs, tiles = features // reps, rows // 128
    noise, target = received(got_ref, ny, features)
    coef, pos_coef = coefficients(query, noise, target, live_ref[...])
    grad = relation * (pos_coef * target + product(noise, coef))
    grad = pick(grad, one_hot(src_ref[...], rows), NT, 2)
    for r in range(reps):
        for t in range(tiles):
            at = (r * tiles + t) * fs
            out_ref[at : at + fs] = grad[r * fs : (r + 1) * fs, t * 128 : (t + 1) * 128]


def update_kernel(reps, grad_ref, et_ref, state_ref, entity_ref, new_state_ref):
    features, rows = et_ref.shape
    fs, tiles = features // reps, rows // 128
    for t in range(tiles):
        lanes = slice(t * 128, (t + 1) * 128)
        grads = [grad_ref[(r * tiles + t) * fs : (r * tiles + t + 1) * fs] for r in range(reps)]
        squares = sum(jnp.sum(grad * grad, axis=0, keepdims=True) for grad in grads)
        state = state_ref[:, lanes] + squares * (1.0 / features)
        new_state_ref[:, lanes] = state
        scale = LEARN_RATE / jnp.sqrt(state)
        for r, grad in enumerate(grads):
            at = slice(r * fs, (r + 1) * fs)
            entity_ref[at, lanes] = et_ref[at, lanes] - grad * scale


def floats(*shapes):
    return [(shape, F32) for shape in shapes]


def call(kernel, outs, *args, scratch=(), flops=0, inputs=pltpu.VMEM, outputs=pltpu.VMEM):
    make = pltpu.HBM if outputs == pltpu.HBM else jax.ShapeDtypeStruct
    shapes = [make(shape, dtype) for shape, dtype in outs]
    moved = sum(4 * a.size for a in args) + sum(4 * math.prod(shape) for shape, _ in outs)
    return pl.pallas_call(
        kernel,
        out_shape=shapes,
        in_specs=[pl.BlockSpec(memory_space=inputs)] * len(args),
        out_specs=[pl.BlockSpec(memory_space=outputs)] * len(outs),
        scratch_shapes=list(scratch),
        cost_estimate=pl.CostEstimate(flops=flops, bytes_accessed=moved, transcendentals=0),
        compiler_params=pltpu.CompilerParams(vmem_limit_bytes=48 << 20),
    )(*args)


def scatter_over_chips(blocks):
    reps = blocks.shape[0]
    chips = reps // 2
    me = lax.axis_index("rep")
    chip, core = me >> 1, me & 1
    pairs = blocks.reshape(chips, 2, *blocks.shape[1:])
    given = lax.dynamic_index_in_dim(pairs, 1 - core, 1, keepdims=False)
    kept = lax.dynamic_index_in_dim(pairs, core, 1, keepdims=False)
    kept = kept + lax.ppermute(given, "rep", [(i, i ^ 1) for i in range(reps)])
    total = lax.dynamic_index_in_dim(kept, chip, 0, keepdims=False)
    for step in range(1, chips):
        given = lax.dynamic_index_in_dim(kept, (chip + step) & (chips - 1), 0, keepdims=False)
        total = total + lax.ppermute(given, "rep", [(i, (i + 2 * step) % reps) for i in range(reps)])
    return total


def per_device(entity, adagrad_state, relation, src_rows, dst_rows, rel_ids, bucket_counts, noise_rows):
    nh, nl, ny, reps = (lax.axis_size(name) for name in ("h", "l", "y", "rep"))
    near = ("l", "y", "rep")
    devices = nl * ny * reps
    rows, features = entity.shape
    slots = src_rows.shape[3]
    edges = nh * nl * ny * slots
    fs, tiles = features // reps, rows // 128
    packed = tiles * fs

    et = entity.T
    mine = lax.dynamic_slice_in_dim(et, lax.axis_index("rep") * fs, fs, 0)
    table = lax.all_gather(mine.reshape(packed, 128), "h").reshape(nh * packed, 128)

    def turned(ids):
        return ids.reshape(nh * nl * ny, slots).T

    given = [turned(ids) for ids in (src_rows, rel_ids, dst_rows)]
    given += [noise_rows.reshape(1, edges), bucket_counts.reshape(1, -1)]
    row = ((1, edges), jnp.int32)
    src, rel, live, wanted = call(
        functools.partial(order_kernel, nh, nl, ny),
        [row, row, ((1, edges), F32), ((devices, 2 * nh * slots), jnp.int32)],
        *(pltpu.with_memory_space_constraint(a, pltpu.HBM) for a in given),
        scratch=[pltpu.VMEM(a.shape, a.dtype) for a in given] + [pltpu.SemaphoreType.DMA((len(given),))],
        inputs=pltpu.HBM,
    )
    asked = lax.all_to_all(wanted, near, split_axis=0, concat_axis=0, tiled=True)
    asked = asked.reshape(devices, 2, nh, slots).transpose(2, 1, 0, 3).reshape(nh, 1, -1)
    relt = relation.T

    unit = 2 * edges * features * rows
    span = 2 * nh * slots
    message = (devices * fs, span)
    wire = (devices, fs // 2, 2, span)
    held = round_up(fs, 8)
    got_shape = pltpu.VMEM((nh, held, 2 * devices * slots), F32)
    (found,) = call(
        functools.partial(table_kernel, fs),
        floats(message),
        table, asked,
        scratch=[got_shape, pltpu.VMEM((3 * held, rows), F32)],
        flops=8 * unit,
    )
    got = lax.all_to_all(found.reshape(wire), near, split_axis=0, concat_axis=0, tiled=True).reshape(message)
    edge_args = (got, et, relt, src, rel, live)
    (terms,) = call(functools.partial(terms_kernel, ny), floats(message), *edge_args, flops=11 * unit)
    terms = lax.all_to_all(terms.reshape(wire), near, split_axis=0, concat_axis=0, tiled=True).reshape(message)
    (partial,) = call(
        functools.partial(scatter_kernel, fs),
        floats((nh, packed, 128)),
        terms, asked,
        scratch=[got_shape, pltpu.VMEM((nh, packed, 128), F32), pltpu.SemaphoreType.DMA((nh,))],
        flops=8 * unit,
        outputs=pltpu.HBM,
    )
    (source,) = call(
        functools.partial(source_kernel, ny, reps), floats((reps * packed, 128)), *edge_args, flops=13 * unit
    )
    partial = lax.all_to_all(partial, "h", split_axis=0, concat_axis=0, tiled=True)
    grad = jnp.sum(partial, axis=0) + scatter_over_chips(source.reshape(reps, packed, 128))
    summed = lax.all_gather(grad, "rep").reshape(reps * packed, 128)
    new_entity, new_state = call(
        functools.partial(update_kernel, reps),
        floats((features, rows), (1, rows)),
        summed, et, adagrad_state.reshape(1, rows),
    )
    return new_entity.T, new_state.reshape(rows)


def solution(mesh):
    dom, reps = mesh.devices.shape
    ny = 4 if dom >= 16 else 2
    axes = ("h", "l", "y", "rep")
    cut = Mesh(mesh.devices.reshape(dom // (2 * ny), 2, ny, reps), axes)
    part = axes[:3]
    return jax.shard_map(
        per_device,
        mesh=cut,
        in_specs=(
            P(part, None),
            P(part),
            P(),
            P(part, "rep", None, None),
            P(part, "rep", None, None),
            P(part, "rep", None, None),
            P(part, "rep", None),
            P(part, "rep", None),
        ),
        out_specs=(P(part, None), P(part)),
        check_vma=False,
    )
```

```python
import functools
import math

import jax
import jax.numpy as jnp
from jax import lax
from jax.experimental import pallas as pl
from jax.experimental.pallas import tpu as pltpu
from jax.sharding import Mesh
from jax.sharding import PartitionSpec as P

LEARN_RATE = 0.3
F32 = jnp.float32
BF16 = jnp.bfloat16
NN = (((1,), (0,)), ((), ()))
NT = (((1,), (1,)), ((), ()))


def round_up(value, unit):
    return -(-value // unit) * unit


def one_hot(row, rows):
    place = lax.broadcasted_iota(jnp.int32, (rows, row.shape[1]), 0)
    return (place == row).astype(F32).astype(BF16)


def split(x, terms):
    out = []
    for _ in range(terms):
        part = x.astype(BF16)
        out.append(part)
        x = x - part.astype(F32)
    return out


def mul(a, b, dims=NN):
    return lax.dot_general(a, b, dims, preferred_element_type=F32)


def pick(x, hot, dims=NN, terms=3):
    n = x.shape[0]
    parts = [part.astype(F32) for part in split(x, terms)]
    out = mul(jnp.concatenate(parts, axis=0).astype(BF16), hot, dims)
    return sum(out[i * n : (i + 1) * n] for i in range(terms - 1, -1, -1))


def product(a, b, dims=NN):
    a_high, a_low = split(a, 2)
    b_high, b_low = split(b, 2)
    return mul(a_low, b_high, dims) + mul(a_high, b_low, dims) + mul(a_high, b_high, dims)


def skewed(v, block):
    n = len(v)
    k = 1
    while k < n:
        high = (block & k) != 0
        v = [jnp.where(high, v[(i + k) % n], v[i]) for i in range(n)]
        k *= 2
    return [v[-i % n] for i in range(n)]


def rotated(row, blocks, span, slots):
    parts = [row[:, i * span : (i + 1) * span] for i in range(row.shape[1] // span)]
    parts = [pltpu.roll(part, shift * slots, 1) if shift else part for part, shift in zip(parts, blocks)]
    return jnp.concatenate(parts, axis=1)


def turned_ids(ids_ref, h, nh, span, slots):
    row = ids_ref[h]
    each = row.shape[1] // (2 * span)
    return rotated(row, [kind * nh + h for kind in range(2) for _ in range(each)], span, slots)


def order_kernel(nh, nl, ny, *refs):
    given, (src_out, rel_out, live_out, wanted_ref), held, sems = refs[:5], refs[5:9], refs[9:14], refs[14]
    copies = [pltpu.make_async_copy(a, b, sems.at[i]) for i, (a, b) in enumerate(zip(given, held))]
    for copy in copies:
        copy.start()
    for copy in copies:
        copy.wait()
    src_ref, rel_ref, dst_ref, noise_ref, count_ref = held
    slots, parts = src_ref.shape
    edges = parts * slots
    lane = lax.broadcasted_iota(jnp.int32, (1, edges), 1)
    slot, group = lane % slots, lane // slots
    h, l, y = group % nh, group // nh % nl, group // (nh * nl)
    part = (h * nl + l) * ny + y
    here = one_hot(part, parts)
    stack = jnp.concatenate([src_ref[...], rel_ref[...], dst_ref[...]], axis=0).astype(F32)
    spread = pick(stack, here, terms=2)
    row = lax.broadcasted_iota(jnp.int32, (slots, edges), 0)

    def own(i):
        mine = jnp.where(row == slot, spread[i * slots : (i + 1) * slots], 0.0)
        return jnp.sum(mine, axis=0, keepdims=True).astype(jnp.int32)

    src_out[...] = own(0)
    rel_out[...] = own(1)
    target = own(2)
    wide = jnp.broadcast_to(noise_ref[...].astype(F32), (8, edges))
    noise = pick(wide, one_hot(part * slots + slot, edges), terms=2)[:1].astype(jnp.int32)
    wide = jnp.broadcast_to(count_ref[...].astype(F32), (8, parts))
    count = mul(wide.astype(BF16), here)[:1].astype(jnp.int32)
    live_out[...] = (slot < count).astype(F32)
    devices, span = wanted_ref.shape
    per = devices // (nl * ny)
    low = lax.broadcasted_iota(jnp.int32, (1, span), 1) < span // 2
    for i in range(ny):
        a, b = noise[:, i * span : (i + 1) * span], target[:, i * span : (i + 1) * span]
        first = jnp.where(low, a, pltpu.roll(b, span // 2, 1))
        second = jnp.where(low, pltpu.roll(a, span // 2, 1), b)
        for k, block in enumerate((first, second)):
            wanted_ref[(k * ny + i) * per : (k * ny + i + 1) * per] = jnp.broadcast_to(block, (per, span))


def queries(et_ref, relt_ref, src_ref, rel_ref):
    source = pick(et_ref[...], one_hot(src_ref[...], et_ref.shape[1]))
    relation = pick(relt_ref[...], one_hot(rel_ref[...], relt_ref.shape[1]))
    return source * relation, relation


def chunks(fs):
    return list(range(0, fs - 7, 8)) + ([fs - 8] if fs % 8 else [])


def table_kernel(fs, table_ref, ids_ref, out_ref, got_ref, stack_ref):
    nh, held, lanes = got_ref.shape
    span = out_ref.shape[1]
    devices = out_ref.shape[0] // fs
    tiles = table_ref.shape[0] // (nh * fs)
    n = 2 * nh
    slots = span // n
    terms = stack_ref.shape[0] // held

    for h in range(nh):
        for t in range(tiles):
            rows = table_ref[pl.ds(h * tiles * fs + t, fs, stride=tiles), :]
            for i, part in enumerate(split(rows, terms)):
                stack_ref[i * held : i * held + fs, t * 128 : (t + 1) * 128] = part.astype(F32)
        found = mul(stack_ref[...].astype(BF16), one_hot(turned_ids(ids_ref, h, nh, span, slots), tiles * 128))
        got_ref[h] = sum(found[i * held : (i + 1) * held] for i in range(terms - 1, -1, -1))
    block = lax.broadcasted_iota(jnp.int32, (8, span), 1) // slots

    def turn(tile, carry):
        for f in chunks(fs):
            v = []
            for kind in range(2):
                start = pl.multiple_of((kind * devices + tile * n) * slots, span)
                v += [got_ref[h, f : f + 8, pl.ds(start, span)] for h in range(nh)]
            v = skewed(v, block)
            for i in range(n):
                out_ref[pl.ds((tile * n + i) * fs + f, 8), :] = pltpu.roll(v[i], (n - i) % n * slots, 1) if i else v[i]
        return carry

    lax.fori_loop(0, devices // n, turn, 0)


def scatter_kernel(fs, msg_ref, ids_ref, out_ref, got_ref, sum_ref, sems):
    nh, held, lanes = got_ref.shape
    span = msg_ref.shape[1]
    devices = msg_ref.shape[0] // fs
    tiles = out_ref.shape[1] // fs
    n = 2 * nh
    slots = span // n
    block = lax.broadcasted_iota(jnp.int32, (8, span), 1) // slots

    def turn(tile, carry):
        for f in chunks(fs):
            v = [msg_ref[pl.ds((tile * n + i) * fs + f, 8), :] for i in range(n)]
            v = skewed([pltpu.roll(v[i], i * slots, 1) if i else v[i] for i in range(n)], block)
            for kind in range(2):
                start = pl.multiple_of((kind * devices + tile * n) * slots, span)
                for h in range(nh):
                    got_ref[h, f : f + 8, pl.ds(start, span)] = v[kind * nh + h]
        return carry

    lax.fori_loop(0, devices // n, turn, 0)

    copies = []
    for h in range(nh):
        grad = pick(got_ref[h], one_hot(turned_ids(ids_ref, h, nh, span, slots), tiles * 128), NT, 2)
        for t in range(tiles):
            sum_ref[h, t * fs : (t + 1) * fs] = grad[:fs, t * 128 : (t + 1) * 128]
        copies.append(pltpu.make_async_copy(sum_ref.at[h], out_ref.at[h], sems.at[h]))
        copies[-1].start()
    for copy in copies:
        copy.wait()


def received(got_ref, ny, features):
    span = got_ref.shape[1]
    low = lax.broadcasted_iota(jnp.int32, (1, span), 1) < span // 2
    noise, target = [], []
    for y in range(ny):
        first, second = (got_ref[(l * ny + y) * features : (l * ny + y + 1) * features] for l in range(2))
        noise.append(jnp.where(low, first, pltpu.roll(second, span // 2, 1)))
        target.append(jnp.where(low, pltpu.roll(first, span // 2, 1), second))
    return jnp.concatenate(noise, axis=1), jnp.concatenate(target, axis=1)


def send(msg_ref, ny, noise, target):
    features, span = noise.shape[0], msg_ref.shape[1]
    low = lax.broadcasted_iota(jnp.int32, (1, span), 1) < span // 2
    for y in range(ny):
        a, b = noise[:, y * span : (y + 1) * span], target[:, y * span : (y + 1) * span]
        first = jnp.where(low, a, pltpu.roll(b, span // 2, 1))
        second = jnp.where(low, pltpu.roll(a, span // 2, 1), b)
        for l, block in enumerate((first, second)):
            msg_ref[(l * ny + y) * features : (l * ny + y + 1) * features] = block


def coefficients(query, noise, target, live):
    coef = jax.nn.sigmoid(product(noise.T, query)) * live
    positive = jnp.sum(query * target, axis=0, keepdims=True)
    return coef, -jax.nn.sigmoid(-positive) * live


def terms_kernel(ny, got_ref, et_ref, relt_ref, src_ref, rel_ref, live_ref, msg_ref):
    query, _ = queries(et_ref, relt_ref, src_ref, rel_ref)
    noise, target = received(got_ref, ny, query.shape[0])
    coef, pos_coef = coefficients(query, noise, target, live_ref[...])
    send(msg_ref, ny, product(query, coef, NT), pos_coef * query)


def source_kernel(ny, reps, got_ref, et_ref, relt_ref, src_ref, rel_ref, live_ref, out_ref):
    query, relation = queries(et_ref, relt_ref, src_ref, rel_ref)
    features, rows = et_ref.shape
    fs, tiles = features // reps, rows // 128
    noise, target = received(got_ref, ny, features)
    coef, pos_coef = coefficients(query, noise, target, live_ref[...])
    grad = relation * (pos_coef * target + product(noise, coef))
    grad = pick(grad, one_hot(src_ref[...], rows), NT, 2)
    for r in range(reps):
        for t in range(tiles):
            at = (r * tiles + t) * fs
            out_ref[at : at + fs] = grad[r * fs : (r + 1) * fs, t * 128 : (t + 1) * 128]


def update_kernel(reps, grad_ref, et_ref, state_ref, entity_ref, new_state_ref):
    features, rows = et_ref.shape
    fs, tiles = features // reps, rows // 128
    for t in range(tiles):
        lanes = slice(t * 128, (t + 1) * 128)
        grads = [grad_ref[(r * tiles + t) * fs : (r * tiles + t + 1) * fs] for r in range(reps)]
        squares = sum(jnp.sum(grad * grad, axis=0, keepdims=True) for grad in grads)
        state = state_ref[:, lanes] + squares * (1.0 / features)
        new_state_ref[:, lanes] = state
        scale = LEARN_RATE / jnp.sqrt(state)
        for r, grad in enumerate(grads):
            at = slice(r * fs, (r + 1) * fs)
            entity_ref[at, lanes] = et_ref[at, lanes] - grad * scale


def floats(*shapes):
    return [(shape, F32) for shape in shapes]


def call(kernel, outs, *args, scratch=(), flops=0, inputs=pltpu.VMEM, outputs=pltpu.VMEM):
    make = pltpu.HBM if outputs == pltpu.HBM else jax.ShapeDtypeStruct
    shapes = [make(shape, dtype) for shape, dtype in outs]
    moved = sum(4 * a.size for a in args) + sum(4 * math.prod(shape) for shape, _ in outs)
    return pl.pallas_call(
        kernel,
        out_shape=shapes,
        in_specs=[pl.BlockSpec(memory_space=inputs)] * len(args),
        out_specs=[pl.BlockSpec(memory_space=outputs)] * len(outs),
        scratch_shapes=list(scratch),
        cost_estimate=pl.CostEstimate(flops=flops, bytes_accessed=moved, transcendentals=0),
        compiler_params=pltpu.CompilerParams(vmem_limit_bytes=48 << 20),
    )(*args)


def scatter_over_chips(blocks):
    reps = blocks.shape[0]
    chips = reps // 2
    me = lax.axis_index("rep")
    chip, core = me >> 1, me & 1
    pairs = blocks.reshape(chips, 2, *blocks.shape[1:])
    given = lax.dynamic_index_in_dim(pairs, 1 - core, 1, keepdims=False)
    kept = lax.dynamic_index_in_dim(pairs, core, 1, keepdims=False)
    kept = kept + lax.ppermute(given, "rep", [(i, i ^ 1) for i in range(reps)])
    total = lax.dynamic_index_in_dim(kept, chip, 0, keepdims=False)
    for step in range(1, chips):
        given = lax.dynamic_index_in_dim(kept, (chip + step) & (chips - 1), 0, keepdims=False)
        total = total + lax.ppermute(given, "rep", [(i, (i + 2 * step) % reps) for i in range(reps)])
    return total


def per_device(entity, adagrad_state, relation, src_rows, dst_rows, rel_ids, bucket_counts, noise_rows):
    nh, nl, ny, reps = (lax.axis_size(name) for name in ("h", "l", "y", "rep"))
    near = ("l", "y", "rep")
    devices = nl * ny * reps
    rows, features = entity.shape
    slots = src_rows.shape[3]
    edges = nh * nl * ny * slots
    fs, tiles = features // reps, rows // 128
    packed = tiles * fs

    et = entity.T
    mine = lax.dynamic_slice_in_dim(et, lax.axis_index("rep") * fs, fs, 0)
    table = lax.all_gather(mine.reshape(packed, 128), "h").reshape(nh * packed, 128)

    def turned(ids):
        return ids.reshape(nh * nl * ny, slots).T

    given = [turned(ids) for ids in (src_rows, rel_ids, dst_rows)]
    given += [noise_rows.reshape(1, edges), bucket_counts.reshape(1, -1)]
    row = ((1, edges), jnp.int32)
    src, rel, live, wanted = call(
        functools.partial(order_kernel, nh, nl, ny),
        [row, row, ((1, edges), F32), ((devices, 2 * nh * slots), jnp.int32)],
        *(pltpu.with_memory_space_constraint(a, pltpu.HBM) for a in given),
        scratch=[pltpu.VMEM(a.shape, a.dtype) for a in given] + [pltpu.SemaphoreType.DMA((len(given),))],
        inputs=pltpu.HBM,
    )
    asked = lax.all_to_all(wanted, near, split_axis=0, concat_axis=0, tiled=True)
    asked = asked.reshape(devices, 2, nh, slots).transpose(2, 1, 0, 3).reshape(nh, 1, -1)
    relt = relation.T

    unit = 2 * edges * features * rows
    span = 2 * nh * slots
    message = (devices * fs, span)
    wire = (devices, fs // 2, 2, span)
    held = round_up(fs, 8)
    got_shape = pltpu.VMEM((nh, held, 2 * devices * slots), F32)
    (found,) = call(
        functools.partial(table_kernel, fs),
        floats(message),
        table, asked,
        scratch=[got_shape, pltpu.VMEM((3 * held, rows), F32)],
        flops=8 * unit,
    )
    got = lax.all_to_all(found.reshape(wire), near, split_axis=0, concat_axis=0, tiled=True).reshape(message)
    edge_args = (got, et, relt, src, rel, live)
    (terms,) = call(functools.partial(terms_kernel, ny), floats(message), *edge_args, flops=11 * unit)
    terms = lax.all_to_all(terms.reshape(wire), near, split_axis=0, concat_axis=0, tiled=True).reshape(message)
    (partial,) = call(
        functools.partial(scatter_kernel, fs),
        floats((nh, packed, 128)),
        terms, asked,
        scratch=[got_shape, pltpu.VMEM((nh, packed, 128), F32), pltpu.SemaphoreType.DMA((nh,))],
        flops=8 * unit,
        outputs=pltpu.HBM,
    )
    (source,) = call(
        functools.partial(source_kernel, ny, reps), floats((reps * packed, 128)), *edge_args, flops=13 * unit
    )
    partial = lax.all_to_all(partial, "h", split_axis=0, concat_axis=0, tiled=True)
    grad = jnp.sum(partial, axis=0) + scatter_over_chips(source.reshape(reps, packed, 128))
    summed = lax.all_gather(grad, "rep").reshape(reps * packed, 128)
    new_entity, new_state = call(
        functools.partial(update_kernel, reps),
        floats((features, rows), (1, rows)),
        summed, et, adagrad_state.reshape(1, rows),
    )
    return new_entity.T, new_state.reshape(rows)


def solution(mesh):
    dom, reps = mesh.devices.shape
    ny = 4 if dom >= 16 else 2
    axes = ("h", "l", "y", "rep")
    cut = Mesh(mesh.devices.reshape(dom // (2 * ny), 2, ny, reps), axes)
    part = axes[:3]
    return jax.shard_map(
        per_device,
        mesh=cut,
        in_specs=(
            P(part, None),
            P(part),
            P(),
            P(part, "rep", None, None),
            P(part, "rep", None, None),
            P(part, "rep", None, None),
            P(part, "rep", None),
            P(part, "rep", None),
        ),
        out_specs=(P(part, None), P(part)),
        check_vma=False,
    )
```

```python
import functools
import math

import jax
import jax.numpy as jnp
from jax import lax
from jax.experimental import pallas as pl
from jax.experimental.pallas import tpu as pltpu
from jax.sharding import Mesh
from jax.sharding import PartitionSpec as P

LEARN_RATE = 0.3
F32 = jnp.float32
BF16 = jnp.bfloat16
NN = (((1,), (0,)), ((), ()))
NT = (((1,), (1,)), ((), ()))


def round_up(value, unit):
    return -(-value // unit) * unit


def one_hot(row, rows):
    place = lax.broadcasted_iota(jnp.int32, (rows, row.shape[1]), 0)
    return (place == row).astype(F32).astype(BF16)


def split(x, terms):
    out = []
    for _ in range(terms):
        part = x.astype(BF16)
        out.append(part)
        x = x - part.astype(F32)
    return out


def mul(a, b, dims=NN):
    return lax.dot_general(a, b, dims, preferred_element_type=F32)


def pick(x, hot, dims=NN, terms=3):
    n = x.shape[0]
    parts = [part.astype(F32) for part in split(x, terms)]
    out = mul(jnp.concatenate(parts, axis=0).astype(BF16), hot, dims)
    return sum(out[i * n : (i + 1) * n] for i in range(terms - 1, -1, -1))


def product(a, b, dims=NN):
    a_high, a_low = split(a, 2)
    b_high, b_low = split(b, 2)
    return mul(a_low, b_high, dims) + mul(a_high, b_low, dims) + mul(a_high, b_high, dims)


def skewed(v, block):
    n = len(v)
    k = 1
    while k < n:
        high = (block & k) != 0
        v = [jnp.where(high, v[(i + k) % n], v[i]) for i in range(n)]
        k *= 2
    return [v[-i % n] for i in range(n)]


def rotated(row, blocks, span, slots):
    parts = [row[:, i * span : (i + 1) * span] for i in range(row.shape[1] // span)]
    parts = [pltpu.roll(part, shift * slots, 1) if shift else part for part, shift in zip(parts, blocks)]
    return jnp.concatenate(parts, axis=1)


def turned_ids(ids_ref, h, nh, span, slots):
    row = ids_ref[h]
    each = row.shape[1] // (2 * span)
    return rotated(row, [kind * nh + h for kind in range(2) for _ in range(each)], span, slots)


def order_kernel(nh, nl, ny, *refs):
    given, (src_out, rel_out, live_out, wanted_ref), held, sems = refs[:5], refs[5:9], refs[9:14], refs[14]
    copies = [pltpu.make_async_copy(a, b, sems.at[i]) for i, (a, b) in enumerate(zip(given, held))]
    for copy in copies:
        copy.start()
    for copy in copies:
        copy.wait()
    src_ref, rel_ref, dst_ref, noise_ref, count_ref = held
    slots, parts = src_ref.shape
    edges = parts * slots
    lane = lax.broadcasted_iota(jnp.int32, (1, edges), 1)
    slot, group = lane % slots, lane // slots
    h, g, y = group % nh, group // nh % nl, group // (nh * nl)
    l = jnp.where(h >= nh // 2, nl - 1 - g, g)
    part = (h * nl + l) * ny + y
    here = one_hot(part, parts)
    stack = jnp.concatenate([src_ref[...], rel_ref[...], dst_ref[...]], axis=0).astype(F32)
    spread = pick(stack, here, terms=2)
    row = lax.broadcasted_iota(jnp.int32, (slots, edges), 0)

    def own(i):
        mine = jnp.where(row == slot, spread[i * slots : (i + 1) * slots], 0.0)
        return jnp.sum(mine, axis=0, keepdims=True).astype(jnp.int32)

    src_out[...] = own(0)
    rel_out[...] = own(1)
    target = own(2)
    wide = jnp.broadcast_to(noise_ref[...].astype(F32), (8, edges))
    noise = pick(wide, one_hot(part * slots + slot, edges), terms=2)[:1].astype(jnp.int32)
    wide = jnp.broadcast_to(count_ref[...].astype(F32), (8, parts))
    count = mul(wide.astype(BF16), here)[:1].astype(jnp.int32)
    live_out[...] = (slot < count).astype(F32)
    devices, span = wanted_ref.shape
    per = devices // (nl * ny)
    low = lax.broadcasted_iota(jnp.int32, (1, span), 1) < span // 2
    for i in range(ny):
        a, b = noise[:, i * span : (i + 1) * span], target[:, i * span : (i + 1) * span]
        first = jnp.where(low, a, pltpu.roll(b, span // 2, 1))
        second = jnp.where(low, pltpu.roll(a, span // 2, 1), b)
        for k, block in enumerate((first, second)):
            wanted_ref[(k * ny + i) * per : (k * ny + i + 1) * per] = jnp.broadcast_to(block, (per, span))


def queries(et_ref, relt_ref, src_ref, rel_ref):
    source = pick(et_ref[...], one_hot(src_ref[...], et_ref.shape[1]))
    relation = pick(relt_ref[...], one_hot(rel_ref[...], relt_ref.shape[1]))
    return source * relation, relation


def chunks(fs):
    return list(range(0, fs - 7, 8)) + ([fs - 8] if fs % 8 else [])


def table_kernel(fs, table_ref, ids_ref, out_ref, got_ref, stack_ref):
    nh, held, lanes = got_ref.shape
    span = out_ref.shape[1]
    devices = out_ref.shape[0] // fs
    tiles = table_ref.shape[0] // (nh * fs)
    n = 2 * nh
    slots = span // n
    terms = stack_ref.shape[0] // held

    for h in range(nh):
        for t in range(tiles):
            rows = table_ref[pl.ds(h * tiles * fs + t, fs, stride=tiles), :]
            for i, part in enumerate(split(rows, terms)):
                stack_ref[i * held : i * held + fs, t * 128 : (t + 1) * 128] = part.astype(F32)
        found = mul(stack_ref[...].astype(BF16), one_hot(turned_ids(ids_ref, h, nh, span, slots), tiles * 128))
        got_ref[h] = sum(found[i * held : (i + 1) * held] for i in range(terms - 1, -1, -1))
    block = lax.broadcasted_iota(jnp.int32, (8, span), 1) // slots

    def turn(tile, carry):
        for f in chunks(fs):
            v = []
            for kind in range(2):
                start = pl.multiple_of((kind * devices + tile * n) * slots, span)
                v += [got_ref[h, f : f + 8, pl.ds(start, span)] for h in range(nh)]
            v = skewed(v, block)
            for i in range(n):
                out_ref[pl.ds((tile * n + i) * fs + f, 8), :] = pltpu.roll(v[i], (n - i) % n * slots, 1) if i else v[i]
        return carry

    lax.fori_loop(0, devices // n, turn, 0)


def scatter_kernel(fs, msg_ref, ids_ref, out_ref, got_ref, sum_ref, sems):
    nh, held, lanes = got_ref.shape
    span = msg_ref.shape[1]
    devices = msg_ref.shape[0] // fs
    tiles = out_ref.shape[1] // fs
    n = 2 * nh
    slots = span // n
    block = lax.broadcasted_iota(jnp.int32, (8, span), 1) // slots

    def turn(tile, carry):
        for f in chunks(fs):
            v = [msg_ref[pl.ds((tile * n + i) * fs + f, 8), :] for i in range(n)]
            v = skewed([pltpu.roll(v[i], i * slots, 1) if i else v[i] for i in range(n)], block)
            for kind in range(2):
                start = pl.multiple_of((kind * devices + tile * n) * slots, span)
                for h in range(nh):
                    got_ref[h, f : f + 8, pl.ds(start, span)] = v[kind * nh + h]
        return carry

    lax.fori_loop(0, devices // n, turn, 0)

    copies = []
    for h in range(nh):
        grad = pick(got_ref[h], one_hot(turned_ids(ids_ref, h, nh, span, slots), tiles * 128), NT, 2)
        for t in range(tiles):
            sum_ref[h, t * fs : (t + 1) * fs] = grad[:fs, t * 128 : (t + 1) * 128]
        copies.append(pltpu.make_async_copy(sum_ref.at[h], out_ref.at[h], sems.at[h]))
        copies[-1].start()
    for copy in copies:
        copy.wait()


def received(got_ref, ny, features):
    span = got_ref.shape[1]
    low = lax.broadcasted_iota(jnp.int32, (1, span), 1) < span // 2
    noise, target = [], []
    for y in range(ny):
        first, second = (got_ref[(l * ny + y) * features : (l * ny + y + 1) * features] for l in range(2))
        noise.append(jnp.where(low, first, pltpu.roll(second, span // 2, 1)))
        target.append(jnp.where(low, pltpu.roll(first, span // 2, 1), second))
    return jnp.concatenate(noise, axis=1), jnp.concatenate(target, axis=1)


def send(msg_ref, ny, noise, target):
    features, span = noise.shape[0], msg_ref.shape[1]
    low = lax.broadcasted_iota(jnp.int32, (1, span), 1) < span // 2
    for y in range(ny):
        a, b = noise[:, y * span : (y + 1) * span], target[:, y * span : (y + 1) * span]
        first = jnp.where(low, a, pltpu.roll(b, span // 2, 1))
        second = jnp.where(low, pltpu.roll(a, span // 2, 1), b)
        for l, block in enumerate((first, second)):
            msg_ref[(l * ny + y) * features : (l * ny + y + 1) * features] = block


def coefficients(query, noise, target, live):
    coef = jax.nn.sigmoid(product(noise.T, query)) * live
    positive = jnp.sum(query * target, axis=0, keepdims=True)
    return coef, -jax.nn.sigmoid(-positive) * live


def terms_kernel(ny, got_ref, et_ref, relt_ref, src_ref, rel_ref, live_ref, msg_ref):
    query, _ = queries(et_ref, relt_ref, src_ref, rel_ref)
    noise, target = received(got_ref, ny, query.shape[0])
    coef, pos_coef = coefficients(query, noise, target, live_ref[...])
    send(msg_ref, ny, product(query, coef, NT), pos_coef * query)


def source_kernel(ny, reps, got_ref, et_ref, relt_ref, src_ref, rel_ref, live_ref, out_ref):
    query, relation = queries(et_ref, relt_ref, src_ref, rel_ref)
    features, rows = et_ref.shape
    fs, tiles = features // reps, rows // 128
    noise, target = received(got_ref, ny, features)
    coef, pos_coef = coefficients(query, noise, target, live_ref[...])
    grad = relation * (pos_coef * target + product(noise, coef))
    grad = pick(grad, one_hot(src_ref[...], rows), NT, 2)
    for r in range(reps):
        for t in range(tiles):
            at = (r * tiles + t) * fs
            out_ref[at : at + fs] = grad[r * fs : (r + 1) * fs, t * 128 : (t + 1) * 128]


def update_kernel(reps, grad_ref, et_ref, state_ref, entity_ref, new_state_ref):
    features, rows = et_ref.shape
    fs, tiles = features // reps, rows // 128
    for t in range(tiles):
        lanes = slice(t * 128, (t + 1) * 128)
        grads = [grad_ref[(r * tiles + t) * fs : (r * tiles + t + 1) * fs] for r in range(reps)]
        squares = sum(jnp.sum(grad * grad, axis=0, keepdims=True) for grad in grads)
        state = state_ref[:, lanes] + squares * (1.0 / features)
        new_state_ref[:, lanes] = state
        scale = LEARN_RATE / jnp.sqrt(state)
        for r, grad in enumerate(grads):
            at = slice(r * fs, (r + 1) * fs)
            entity_ref[at, lanes] = et_ref[at, lanes] - grad * scale


def floats(*shapes):
    return [(shape, F32) for shape in shapes]


def call(kernel, outs, *args, scratch=(), flops=0, inputs=pltpu.VMEM, outputs=pltpu.VMEM):
    make = pltpu.HBM if outputs == pltpu.HBM else jax.ShapeDtypeStruct
    shapes = [make(shape, dtype) for shape, dtype in outs]
    moved = sum(4 * a.size for a in args) + sum(4 * math.prod(shape) for shape, _ in outs)
    return pl.pallas_call(
        kernel,
        out_shape=shapes,
        in_specs=[pl.BlockSpec(memory_space=inputs)] * len(args),
        out_specs=[pl.BlockSpec(memory_space=outputs)] * len(outs),
        scratch_shapes=list(scratch),
        cost_estimate=pl.CostEstimate(flops=flops, bytes_accessed=moved, transcendentals=0),
        compiler_params=pltpu.CompilerParams(vmem_limit_bytes=48 << 20),
    )(*args)


def scatter_over_chips(blocks):
    reps = blocks.shape[0]
    chips = reps // 2
    me = lax.axis_index("rep")
    chip, core = me >> 1, me & 1
    pairs = blocks.reshape(chips, 2, *blocks.shape[1:])
    given = lax.dynamic_index_in_dim(pairs, 1 - core, 1, keepdims=False)
    kept = lax.dynamic_index_in_dim(pairs, core, 1, keepdims=False)
    kept = kept + lax.ppermute(given, "rep", [(i, i ^ 1) for i in range(reps)])
    total = lax.dynamic_index_in_dim(kept, chip, 0, keepdims=False)
    for step in range(1, chips):
        given = lax.dynamic_index_in_dim(kept, (chip + step) & (chips - 1), 0, keepdims=False)
        total = total + lax.ppermute(given, "rep", [(i, (i + 2 * step) % reps) for i in range(reps)])
    return total


def groups_of(nh, nl, ny, reps):
    def z(h, g):
        return h * nl + (nl - 1 - g if h >= nh // 2 else g)

    far = [[z(h, g) for h in range(nh)] for g in range(nl)]
    near = [
        [(z(h, g) * ny + y) * reps + r for g in range(nl) for y in range(ny) for r in range(reps)] for h in range(nh)
    ]
    return far, near


def per_device(entity, adagrad_state, relation, src_rows, dst_rows, rel_ids, bucket_counts, noise_rows):
    nh, nl, ny, reps = (lax.axis_size(name) for name in ("h", "l", "y", "rep"))
    far_groups, near_groups = groups_of(nh, nl, ny, reps)

    def exchange(x, names, groups):
        return lax.all_to_all(x, names, split_axis=0, concat_axis=0, axis_index_groups=groups, tiled=True)

    def near(x):
        return exchange(x, ("h", "l", "y", "rep"), near_groups)

    devices = nl * ny * reps
    rows, features = entity.shape
    slots = src_rows.shape[3]
    edges = nh * nl * ny * slots
    fs, tiles = features // reps, rows // 128
    packed = tiles * fs

    et = entity.T
    mine = lax.dynamic_slice_in_dim(et, lax.axis_index("rep") * fs, fs, 0)
    table = lax.all_gather(mine.reshape(packed, 128), ("h", "l"), axis_index_groups=far_groups).reshape(nh * packed, 128)

    def turned(ids):
        return ids.reshape(nh * nl * ny, slots).T

    given = [turned(ids) for ids in (src_rows, rel_ids, dst_rows)]
    given += [noise_rows.reshape(1, edges), bucket_counts.reshape(1, -1)]
    row = ((1, edges), jnp.int32)
    src, rel, live, wanted = call(
        functools.partial(order_kernel, nh, nl, ny),
        [row, row, ((1, edges), F32), ((devices, 2 * nh * slots), jnp.int32)],
        *(pltpu.with_memory_space_constraint(a, pltpu.HBM) for a in given),
        scratch=[pltpu.VMEM(a.shape, a.dtype) for a in given] + [pltpu.SemaphoreType.DMA((len(given),))],
        inputs=pltpu.HBM,
    )
    asked = near(wanted)
    asked = asked.reshape(devices, 2, nh, slots).transpose(2, 1, 0, 3).reshape(nh, 1, -1)
    relt = relation.T

    unit = 2 * edges * features * rows
    span = 2 * nh * slots
    message = (devices * fs, span)
    wire = (devices, fs // 2, 2, span)
    held = round_up(fs, 8)
    got_shape = pltpu.VMEM((nh, held, 2 * devices * slots), F32)
    (found,) = call(
        functools.partial(table_kernel, fs),
        floats(message),
        table, asked,
        scratch=[got_shape, pltpu.VMEM((3 * held, rows), F32)],
        flops=8 * unit,
    )
    got = near(found.reshape(wire)).reshape(message)
    edge_args = (got, et, relt, src, rel, live)
    (terms,) = call(functools.partial(terms_kernel, ny), floats(message), *edge_args, flops=11 * unit)
    terms = near(terms.reshape(wire)).reshape(message)
    (partial,) = call(
        functools.partial(scatter_kernel, fs),
        floats((nh, packed, 128)),
        terms, asked,
        scratch=[got_shape, pltpu.VMEM((nh, packed, 128), F32), pltpu.SemaphoreType.DMA((nh,))],
        flops=8 * unit,
        outputs=pltpu.HBM,
    )
    (source,) = call(
        functools.partial(source_kernel, ny, reps), floats((reps * packed, 128)), *edge_args, flops=13 * unit
    )
    partial = exchange(partial, ("h", "l"), far_groups)
    grad = jnp.sum(partial, axis=0) + scatter_over_chips(source.reshape(reps, packed, 128))
    summed = lax.all_gather(grad, "rep").reshape(reps * packed, 128)
    new_entity, new_state = call(
        functools.partial(update_kernel, reps),
        floats((features, rows), (1, rows)),
        summed, et, adagrad_state.reshape(1, rows),
    )
    return new_entity.T, new_state.reshape(rows)


def solution(mesh):
    dom, reps = mesh.devices.shape
    ny = 4 if dom >= 16 else 2
    axes = ("h", "l", "y", "rep")
    cut = Mesh(mesh.devices.reshape(dom // (2 * ny), 2, ny, reps), axes)
    part = axes[:3]
    return jax.shard_map(
        per_device,
        mesh=cut,
        in_specs=(
            P(part, None),
            P(part),
            P(),
            P(part, "rep", None, None),
            P(part, "rep", None, None),
            P(part, "rep", None, None),
            P(part, "rep", None),
            P(part, "rep", None),
        ),
        out_specs=(P(part, None), P(part)),
        check_vma=False,
    )
```

```python
import functools
import math

import jax
import jax.numpy as jnp
from jax import lax
from jax.experimental import pallas as pl
from jax.experimental.pallas import tpu as pltpu
from jax.sharding import Mesh
from jax.sharding import PartitionSpec as P

LEARN_RATE = 0.3
F32 = jnp.float32
BF16 = jnp.bfloat16
NN = (((1,), (0,)), ((), ()))
NT = (((1,), (1,)), ((), ()))


def round_up(value, unit):
    return -(-value // unit) * unit


def one_hot(row, rows):
    place = lax.broadcasted_iota(jnp.int32, (rows, row.shape[1]), 0)
    return (place == row).astype(F32).astype(BF16)


def split(x, terms):
    out = []
    for _ in range(terms):
        part = x.astype(BF16)
        out.append(part)
        x = x - part.astype(F32)
    return out


def mul(a, b, dims=NN):
    return lax.dot_general(a, b, dims, preferred_element_type=F32)


def pick(x, hot, dims=NN, terms=3):
    n = x.shape[0]
    parts = [part.astype(F32) for part in split(x, terms)]
    out = mul(jnp.concatenate(parts, axis=0).astype(BF16), hot, dims)
    return sum(out[i * n : (i + 1) * n] for i in range(terms - 1, -1, -1))


def product(a, b, dims=NN):
    a_high, a_low = split(a, 2)
    b_high, b_low = split(b, 2)
    return mul(a_low, b_high, dims) + mul(a_high, b_low, dims) + mul(a_high, b_high, dims)


def skewed(v, block):
    n = len(v)
    k = 1
    while k < n:
        high = (block & k) != 0
        v = [jnp.where(high, v[(i + k) % n], v[i]) for i in range(n)]
        k *= 2
    return [v[-i % n] for i in range(n)]


def rotated(row, blocks, span, slots):
    parts = [row[:, i * span : (i + 1) * span] for i in range(row.shape[1] // span)]
    parts = [pltpu.roll(part, shift * slots, 1) if shift else part for part, shift in zip(parts, blocks)]
    return jnp.concatenate(parts, axis=1)


def turned_ids(ids_ref, h, nh, span, slots):
    row = ids_ref[h]
    each = row.shape[1] // (2 * span)
    return rotated(row, [kind * nh + h for kind in range(2) for _ in range(each)], span, slots)


def order_kernel(nh, nl, ny, *refs):
    given, (src_out, rel_out, live_out, wanted_ref), held, sems = refs[:5], refs[5:9], refs[9:14], refs[14]
    copies = [pltpu.make_async_copy(a, b, sems.at[i]) for i, (a, b) in enumerate(zip(given, held))]
    for copy in copies:
        copy.start()
    for copy in copies:
        copy.wait()
    src_ref, rel_ref, dst_ref, noise_ref, count_ref = held
    slots, parts = src_ref.shape
    edges = parts * slots
    lane = lax.broadcasted_iota(jnp.int32, (1, edges), 1)
    slot, group = lane % slots, lane // slots
    h, l, y = group % nh, group // nh % nl, group // (nh * nl)
    part = (h * nl + l) * ny + y
    here = one_hot(part, parts)
    stack = jnp.concatenate([src_ref[...], rel_ref[...], dst_ref[...]], axis=0).astype(F32)
    spread = pick(stack, here, terms=2)
    row = lax.broadcasted_iota(jnp.int32, (slots, edges), 0)

    def own(i):
        mine = jnp.where(row == slot, spread[i * slots : (i + 1) * slots], 0.0)
        return jnp.sum(mine, axis=0, keepdims=True).astype(jnp.int32)

    src_out[...] = own(0)
    rel_out[...] = own(1)
    target = own(2)
    wide = jnp.broadcast_to(noise_ref[...].astype(F32), (8, edges))
    noise = pick(wide, one_hot(part * slots + slot, edges), terms=2)[:1].astype(jnp.int32)
    wide = jnp.broadcast_to(count_ref[...].astype(F32), (8, parts))
    count = mul(wide.astype(BF16), here)[:1].astype(jnp.int32)
    live_out[...] = (slot < count).astype(F32)
    devices, span = wanted_ref.shape
    per = devices // (nl * ny)
    low = lax.broadcasted_iota(jnp.int32, (1, span), 1) < span // 2
    for i in range(ny):
        a, b = noise[:, i * span : (i + 1) * span], target[:, i * span : (i + 1) * span]
        first = jnp.where(low, a, pltpu.roll(b, span // 2, 1))
        second = jnp.where(low, pltpu.roll(a, span // 2, 1), b)
        for k, block in enumerate((first, second)):
            wanted_ref[(k * ny + i) * per : (k * ny + i + 1) * per] = jnp.broadcast_to(block, (per, span))


def queries(et_ref, relt_ref, src_ref, rel_ref):
    source = pick(et_ref[...], one_hot(src_ref[...], et_ref.shape[1]))
    relation = pick(relt_ref[...], one_hot(rel_ref[...], relt_ref.shape[1]))
    return source * relation, relation


def chunks(fs):
    return list(range(0, fs - 7, 8)) + ([fs - 8] if fs % 8 else [])


def table_kernel(fs, table_ref, ids_ref, out_ref, got_ref, stack_ref):
    nh, held, lanes = got_ref.shape
    span = out_ref.shape[1]
    devices = out_ref.shape[0] // fs
    tiles = table_ref.shape[0] // (nh * fs)
    n = 2 * nh
    slots = span // n
    terms = stack_ref.shape[0] // held

    for h in range(nh):
        for t in range(tiles):
            rows = table_ref[pl.ds(h * tiles * fs + t, fs, stride=tiles), :]
            for i, part in enumerate(split(rows, terms)):
                stack_ref[i * held : i * held + fs, t * 128 : (t + 1) * 128] = part.astype(F32)
        found = mul(stack_ref[...].astype(BF16), one_hot(turned_ids(ids_ref, h, nh, span, slots), tiles * 128))
        got_ref[h] = sum(found[i * held : (i + 1) * held] for i in range(terms - 1, -1, -1))
    block = lax.broadcasted_iota(jnp.int32, (8, span), 1) // slots

    def turn(tile, carry):
        for f in chunks(fs):
            v = []
            for kind in range(2):
                start = pl.multiple_of((kind * devices + tile * n) * slots, span)
                v += [got_ref[h, f : f + 8, pl.ds(start, span)] for h in range(nh)]
            v = skewed(v, block)
            for i in range(n):
                out_ref[pl.ds((tile * n + i) * fs + f, 8), :] = pltpu.roll(v[i], (n - i) % n * slots, 1) if i else v[i]
        return carry

    lax.fori_loop(0, devices // n, turn, 0)


def scatter_kernel(fs, msg_ref, ids_ref, out_ref, got_ref, sum_ref, sems):
    nh, held, lanes = got_ref.shape
    span = msg_ref.shape[1]
    devices = msg_ref.shape[0] // fs
    tiles = out_ref.shape[1] // fs
    n = 2 * nh
    slots = span // n
    block = lax.broadcasted_iota(jnp.int32, (8, span), 1) // slots

    def turn(tile, carry):
        for f in chunks(fs):
            v = [msg_ref[pl.ds((tile * n + i) * fs + f, 8), :] for i in range(n)]
            v = skewed([pltpu.roll(v[i], i * slots, 1) if i else v[i] for i in range(n)], block)
            for kind in range(2):
                start = pl.multiple_of((kind * devices + tile * n) * slots, span)
                for h in range(nh):
                    got_ref[h, f : f + 8, pl.ds(start, span)] = v[kind * nh + h]
        return carry

    lax.fori_loop(0, devices // n, turn, 0)

    copies = []
    for h in range(nh):
        grad = pick(got_ref[h], one_hot(turned_ids(ids_ref, h, nh, span, slots), tiles * 128), NT, 2)
        for t in range(tiles):
            sum_ref[h, t * fs : (t + 1) * fs] = grad[:fs, t * 128 : (t + 1) * 128]
        copies.append(pltpu.make_async_copy(sum_ref.at[h], out_ref.at[h], sems.at[h]))
        copies[-1].start()
    for copy in copies:
        copy.wait()


def received(got_ref, ny, features):
    span = got_ref.shape[1]
    low = lax.broadcasted_iota(jnp.int32, (1, span), 1) < span // 2
    noise, target = [], []
    for y in range(ny):
        first, second = (got_ref[(l * ny + y) * features : (l * ny + y + 1) * features] for l in range(2))
        noise.append(jnp.where(low, first, pltpu.roll(second, span // 2, 1)))
        target.append(jnp.where(low, pltpu.roll(first, span // 2, 1), second))
    return jnp.concatenate(noise, axis=1), jnp.concatenate(target, axis=1)


def send(msg_ref, ny, noise, target):
    features, span = noise.shape[0], msg_ref.shape[1]
    low = lax.broadcasted_iota(jnp.int32, (1, span), 1) < span // 2
    for y in range(ny):
        a, b = noise[:, y * span : (y + 1) * span], target[:, y * span : (y + 1) * span]
        first = jnp.where(low, a, pltpu.roll(b, span // 2, 1))
        second = jnp.where(low, pltpu.roll(a, span // 2, 1), b)
        for l, block in enumerate((first, second)):
            msg_ref[(l * ny + y) * features : (l * ny + y + 1) * features] = block


def coefficients(query, noise, target, live):
    coef = jax.nn.sigmoid(product(noise.T, query)) * live
    positive = jnp.sum(query * target, axis=0, keepdims=True)
    return coef, -jax.nn.sigmoid(-positive) * live


def terms_kernel(ny, got_ref, et_ref, relt_ref, src_ref, rel_ref, live_ref, msg_ref):
    query, _ = queries(et_ref, relt_ref, src_ref, rel_ref)
    noise, target = received(got_ref, ny, query.shape[0])
    coef, pos_coef = coefficients(query, noise, target, live_ref[...])
    send(msg_ref, ny, product(query, coef, NT), pos_coef * query)


def source_kernel(ny, reps, got_ref, et_ref, relt_ref, src_ref, rel_ref, live_ref, out_ref):
    query, relation = queries(et_ref, relt_ref, src_ref, rel_ref)
    features, rows = et_ref.shape
    fs, tiles = features // reps, rows // 128
    noise, target = received(got_ref, ny, features)
    coef, pos_coef = coefficients(query, noise, target, live_ref[...])
    grad = relation * (pos_coef * target + product(noise, coef))
    grad = pick(grad, one_hot(src_ref[...], rows), NT, 2)
    for r in range(reps):
        for t in range(tiles):
            at = (r * tiles + t) * fs
            out_ref[at : at + fs] = grad[r * fs : (r + 1) * fs, t * 128 : (t + 1) * 128]


def update_kernel(reps, grad_ref, et_ref, state_ref, entity_ref, new_state_ref):
    features, rows = et_ref.shape
    fs, tiles = features // reps, rows // 128
    for t in range(tiles):
        lanes = slice(t * 128, (t + 1) * 128)
        grads = [grad_ref[(r * tiles + t) * fs : (r * tiles + t + 1) * fs] for r in range(reps)]
        squares = sum(jnp.sum(grad * grad, axis=0, keepdims=True) for grad in grads)
        state = state_ref[:, lanes] + squares * (1.0 / features)
        new_state_ref[:, lanes] = state
        scale = LEARN_RATE / jnp.sqrt(state)
        for r, grad in enumerate(grads):
            at = slice(r * fs, (r + 1) * fs)
            entity_ref[at, lanes] = et_ref[at, lanes] - grad * scale


def floats(*shapes):
    return [(shape, F32) for shape in shapes]


def call(kernel, outs, *args, scratch=(), flops=0, inputs=pltpu.VMEM, outputs=pltpu.VMEM):
    make = pltpu.HBM if outputs == pltpu.HBM else jax.ShapeDtypeStruct
    shapes = [make(shape, dtype) for shape, dtype in outs]
    moved = sum(4 * a.size for a in args) + sum(4 * math.prod(shape) for shape, _ in outs)
    return pl.pallas_call(
        kernel,
        out_shape=shapes,
        in_specs=[pl.BlockSpec(memory_space=inputs)] * len(args),
        out_specs=[pl.BlockSpec(memory_space=outputs)] * len(outs),
        scratch_shapes=list(scratch),
        cost_estimate=pl.CostEstimate(flops=flops, bytes_accessed=moved, transcendentals=0),
        compiler_params=pltpu.CompilerParams(vmem_limit_bytes=48 << 20),
    )(*args)


def scatter_over_chips(blocks):
    reps = blocks.shape[0]
    chips = reps // 2
    me = lax.axis_index("rep")
    chip, core = me >> 1, me & 1
    pairs = blocks.reshape(chips, 2, *blocks.shape[1:])
    given = lax.dynamic_index_in_dim(pairs, 1 - core, 1, keepdims=False)
    kept = lax.dynamic_index_in_dim(pairs, core, 1, keepdims=False)
    kept = kept + lax.ppermute(given, "rep", [(i, i ^ 1) for i in range(reps)])
    total = lax.dynamic_index_in_dim(kept, chip, 0, keepdims=False)
    for step in range(1, chips):
        given = lax.dynamic_index_in_dim(kept, (chip + step) & (chips - 1), 0, keepdims=False)
        total = total + lax.ppermute(given, "rep", [(i, (i + 2 * step) % reps) for i in range(reps)])
    return total


def per_device(entity, adagrad_state, relation, src_rows, dst_rows, rel_ids, bucket_counts, noise_rows):
    nh, nl, ny, reps = (lax.axis_size(name) for name in ("h", "l", "y", "rep"))
    near = ("l", "y", "rep")
    devices = nl * ny * reps
    rows, features = entity.shape
    slots = src_rows.shape[3]
    edges = nh * nl * ny * slots
    fs, tiles = features // reps, rows // 128
    packed = tiles * fs

    et = entity.T
    mine = lax.dynamic_slice_in_dim(et, lax.axis_index("rep") * fs, fs, 0)
    table = lax.all_gather(mine.reshape(packed, 128), "h").reshape(nh * packed, 128)

    def turned(ids):
        return ids.reshape(nh * nl * ny, slots).T

    given = [turned(ids) for ids in (src_rows, rel_ids, dst_rows)]
    given += [noise_rows.reshape(1, edges), bucket_counts.reshape(1, -1)]
    row = ((1, edges), jnp.int32)
    src, rel, live, wanted = call(
        functools.partial(order_kernel, nh, nl, ny),
        [row, row, ((1, edges), F32), ((devices, 2 * nh * slots), jnp.int32)],
        *(pltpu.with_memory_space_constraint(a, pltpu.HBM) for a in given),
        scratch=[pltpu.VMEM(a.shape, a.dtype) for a in given] + [pltpu.SemaphoreType.DMA((len(given),))],
        inputs=pltpu.HBM,
    )
    table, wanted = lax.optimization_barrier((table, wanted))
    asked = lax.all_to_all(wanted, near, split_axis=0, concat_axis=0, tiled=True)
    asked = asked.reshape(devices, 2, nh, slots).transpose(2, 1, 0, 3).reshape(nh, 1, -1)
    relt = relation.T

    unit = 2 * edges * features * rows
    span = 2 * nh * slots
    message = (devices * fs, span)
    wire = (devices, fs // 2, 2, span)
    held = round_up(fs, 8)
    got_shape = pltpu.VMEM((nh, held, 2 * devices * slots), F32)
    (found,) = call(
        functools.partial(table_kernel, fs),
        floats(message),
        table, asked,
        scratch=[got_shape, pltpu.VMEM((3 * held, rows), F32)],
        flops=8 * unit,
    )
    got = lax.all_to_all(found.reshape(wire), near, split_axis=0, concat_axis=0, tiled=True).reshape(message)
    edge_args = (got, et, relt, src, rel, live)
    (terms,) = call(functools.partial(terms_kernel, ny), floats(message), *edge_args, flops=11 * unit)
    terms = lax.all_to_all(terms.reshape(wire), near, split_axis=0, concat_axis=0, tiled=True).reshape(message)
    (partial,) = call(
        functools.partial(scatter_kernel, fs),
        floats((nh, packed, 128)),
        terms, asked,
        scratch=[got_shape, pltpu.VMEM((nh, packed, 128), F32), pltpu.SemaphoreType.DMA((nh,))],
        flops=8 * unit,
        outputs=pltpu.HBM,
    )
    (source,) = call(
        functools.partial(source_kernel, ny, reps), floats((reps * packed, 128)), *edge_args, flops=13 * unit
    )
    partial = lax.all_to_all(partial, "h", split_axis=0, concat_axis=0, tiled=True)
    grad = jnp.sum(partial, axis=0) + scatter_over_chips(source.reshape(reps, packed, 128))
    summed = lax.all_gather(grad, "rep").reshape(reps * packed, 128)
    new_entity, new_state = call(
        functools.partial(update_kernel, reps),
        floats((features, rows), (1, rows)),
        summed, et, adagrad_state.reshape(1, rows),
    )
    return new_entity.T, new_state.reshape(rows)


def solution(mesh):
    dom, reps = mesh.devices.shape
    ny = 4 if dom >= 16 else 2
    axes = ("h", "l", "y", "rep")
    cut = Mesh(mesh.devices.reshape(dom // (2 * ny), 2, ny, reps), axes)
    part = axes[:3]
    return jax.shard_map(
        per_device,
        mesh=cut,
        in_specs=(
            P(part, None),
            P(part),
            P(),
            P(part, "rep", None, None),
            P(part, "rep", None, None),
            P(part, "rep", None, None),
            P(part, "rep", None),
            P(part, "rep", None),
        ),
        out_specs=(P(part, None), P(part)),
        check_vma=False,
    )
```

```python
import functools
import math

import jax
import jax.numpy as jnp
from jax import lax
from jax.experimental import pallas as pl
from jax.experimental.pallas import tpu as pltpu
from jax.sharding import Mesh
from jax.sharding import PartitionSpec as P

LEARN_RATE = 0.3
F32 = jnp.float32
BF16 = jnp.bfloat16
NN = (((1,), (0,)), ((), ()))
NT = (((1,), (1,)), ((), ()))


def round_up(value, unit):
    return -(-value // unit) * unit


def one_hot(row, rows):
    place = lax.broadcasted_iota(jnp.int32, (rows, row.shape[1]), 0)
    return (place == row).astype(F32).astype(BF16)


def split(x, terms):
    out = []
    for _ in range(terms):
        part = x.astype(BF16)
        out.append(part)
        x = x - part.astype(F32)
    return out


def mul(a, b, dims=NN):
    return lax.dot_general(a, b, dims, preferred_element_type=F32)


def pick(x, hot, dims=NN, terms=2):
    n = x.shape[0]
    parts = [part.astype(F32) for part in split(x, terms)]
    out = mul(jnp.concatenate(parts, axis=0).astype(BF16), hot, dims)
    return sum(out[i * n : (i + 1) * n] for i in range(terms - 1, -1, -1))


def product(a, b, dims=NN):
    a_high, a_low = split(a, 2)
    b_high, b_low = split(b, 2)
    return mul(a_low, b_high, dims) + mul(a_high, b_low, dims) + mul(a_high, b_high, dims)


def skewed(v, block):
    n = len(v)
    k = 1
    while k < n:
        high = (block & k) != 0
        v = [jnp.where(high, v[(i + k) % n], v[i]) for i in range(n)]
        k *= 2
    return [v[-i % n] for i in range(n)]


def rotated(row, blocks, span, slots):
    parts = [row[:, i * span : (i + 1) * span] for i in range(row.shape[1] // span)]
    parts = [pltpu.roll(part, shift * slots, 1) if shift else part for part, shift in zip(parts, blocks)]
    return jnp.concatenate(parts, axis=1)


def turned_ids(ids_ref, h, nh, span, slots):
    row = ids_ref[h]
    each = row.shape[1] // (2 * span)
    return rotated(row, [kind * nh + h for kind in range(2) for _ in range(each)], span, slots)


def order_kernel(nh, nl, ny, *refs):
    given, (src_out, rel_out, live_out, wanted_ref), held, sems = refs[:5], refs[5:9], refs[9:14], refs[14]
    copies = [pltpu.make_async_copy(a, b, sems.at[i]) for i, (a, b) in enumerate(zip(given, held))]
    for copy in copies:
        copy.start()
    for copy in copies:
        copy.wait()
    src_ref, rel_ref, dst_ref, noise_ref, count_ref = held
    slots, parts = src_ref.shape
    edges = parts * slots
    lane = lax.broadcasted_iota(jnp.int32, (1, edges), 1)
    slot, group = lane % slots, lane // slots
    h, l, y = group % nh, group // nh % nl, group // (nh * nl)
    part = (h * nl + l) * ny + y
    here = one_hot(part, parts)
    stack = jnp.concatenate([src_ref[...], rel_ref[...], dst_ref[...]], axis=0).astype(F32)
    spread = pick(stack, here, terms=2)
    row = lax.broadcasted_iota(jnp.int32, (slots, edges), 0)

    def own(i):
        mine = jnp.where(row == slot, spread[i * slots : (i + 1) * slots], 0.0)
        return jnp.sum(mine, axis=0, keepdims=True).astype(jnp.int32)

    src_out[...] = own(0)
    rel_out[...] = own(1)
    target = own(2)
    wide = jnp.broadcast_to(noise_ref[...].astype(F32), (8, edges))
    noise = pick(wide, one_hot(part * slots + slot, edges), terms=2)[:1].astype(jnp.int32)
    wide = jnp.broadcast_to(count_ref[...].astype(F32), (8, parts))
    count = mul(wide.astype(BF16), here)[:1].astype(jnp.int32)
    live_out[...] = (slot < count).astype(F32)
    devices, span = wanted_ref.shape
    per = devices // (nl * ny)
    low = lax.broadcasted_iota(jnp.int32, (1, span), 1) < span // 2
    for i in range(ny):
        a, b = noise[:, i * span : (i + 1) * span], target[:, i * span : (i + 1) * span]
        first = jnp.where(low, a, pltpu.roll(b, span // 2, 1))
        second = jnp.where(low, pltpu.roll(a, span // 2, 1), b)
        for k, block in enumerate((first, second)):
            wanted_ref[(k * ny + i) * per : (k * ny + i + 1) * per] = jnp.broadcast_to(block, (per, span))


def queries(et_ref, relt_ref, src_ref, rel_ref):
    source = pick(et_ref[...], one_hot(src_ref[...], et_ref.shape[1]))
    relation = pick(relt_ref[...], one_hot(rel_ref[...], relt_ref.shape[1]))
    return source * relation, relation


def chunks(fs):
    return list(range(0, fs - 7, 8)) + ([fs - 8] if fs % 8 else [])


def table_kernel(fs, table_ref, ids_ref, out_ref, got_ref, stack_ref):
    nh, held, lanes = got_ref.shape
    span = out_ref.shape[1]
    devices = out_ref.shape[0] // fs
    tiles = table_ref.shape[0] // (nh * fs)
    n = 2 * nh
    slots = span // n
    terms = stack_ref.shape[0] // held

    for h in range(nh):
        for t in range(tiles):
            rows = table_ref[pl.ds(h * tiles * fs + t, fs, stride=tiles), :]
            for i, part in enumerate(split(rows, terms)):
                stack_ref[i * held : i * held + fs, t * 128 : (t + 1) * 128] = part.astype(F32)
        found = mul(stack_ref[...].astype(BF16), one_hot(turned_ids(ids_ref, h, nh, span, slots), tiles * 128))
        got_ref[h] = sum(found[i * held : (i + 1) * held] for i in range(terms - 1, -1, -1))
    block = lax.broadcasted_iota(jnp.int32, (8, span), 1) // slots

    def turn(tile, carry):
        for f in chunks(fs):
            v = []
            for kind in range(2):
                start = pl.multiple_of((kind * devices + tile * n) * slots, span)
                v += [got_ref[h, f : f + 8, pl.ds(start, span)] for h in range(nh)]
            v = skewed(v, block)
            for i in range(n):
                out_ref[pl.ds((tile * n + i) * fs + f, 8), :] = pltpu.roll(v[i], (n - i) % n * slots, 1) if i else v[i]
        return carry

    lax.fori_loop(0, devices // n, turn, 0)


def scatter_kernel(fs, msg_ref, ids_ref, out_ref, got_ref, sum_ref, sems):
    nh, held, lanes = got_ref.shape
    span = msg_ref.shape[1]
    devices = msg_ref.shape[0] // fs
    tiles = out_ref.shape[1] // fs
    n = 2 * nh
    slots = span // n
    block = lax.broadcasted_iota(jnp.int32, (8, span), 1) // slots

    def turn(tile, carry):
        for f in chunks(fs):
            v = [msg_ref[pl.ds((tile * n + i) * fs + f, 8), :] for i in range(n)]
            v = skewed([pltpu.roll(v[i], i * slots, 1) if i else v[i] for i in range(n)], block)
            for kind in range(2):
                start = pl.multiple_of((kind * devices + tile * n) * slots, span)
                for h in range(nh):
                    got_ref[h, f : f + 8, pl.ds(start, span)] = v[kind * nh + h]
        return carry

    lax.fori_loop(0, devices // n, turn, 0)

    copies = []
    for h in range(nh):
        grad = pick(got_ref[h], one_hot(turned_ids(ids_ref, h, nh, span, slots), tiles * 128), NT, 2)
        for t in range(tiles):
            sum_ref[h, t * fs : (t + 1) * fs] = grad[:fs, t * 128 : (t + 1) * 128]
        copies.append(pltpu.make_async_copy(sum_ref.at[h], out_ref.at[h], sems.at[h]))
        copies[-1].start()
    for copy in copies:
        copy.wait()


def received(got_ref, ny, features):
    span = got_ref.shape[1]
    low = lax.broadcasted_iota(jnp.int32, (1, span), 1) < span // 2
    noise, target = [], []
    for y in range(ny):
        first, second = (got_ref[(l * ny + y) * features : (l * ny + y + 1) * features] for l in range(2))
        noise.append(jnp.where(low, first, pltpu.roll(second, span // 2, 1)))
        target.append(jnp.where(low, pltpu.roll(first, span // 2, 1), second))
    return jnp.concatenate(noise, axis=1), jnp.concatenate(target, axis=1)


def send(msg_ref, ny, noise, target):
    features, span = noise.shape[0], msg_ref.shape[1]
    low = lax.broadcasted_iota(jnp.int32, (1, span), 1) < span // 2
    for y in range(ny):
        a, b = noise[:, y * span : (y + 1) * span], target[:, y * span : (y + 1) * span]
        first = jnp.where(low, a, pltpu.roll(b, span // 2, 1))
        second = jnp.where(low, pltpu.roll(a, span // 2, 1), b)
        for l, block in enumerate((first, second)):
            msg_ref[(l * ny + y) * features : (l * ny + y + 1) * features] = block


def coefficients(query, noise, target, live):
    coef = jax.nn.sigmoid(product(noise.T, query)) * live
    positive = jnp.sum(query * target, axis=0, keepdims=True)
    return coef, -jax.nn.sigmoid(-positive) * live


def terms_kernel(ny, got_ref, et_ref, relt_ref, src_ref, rel_ref, live_ref, msg_ref):
    query, _ = queries(et_ref, relt_ref, src_ref, rel_ref)
    noise, target = received(got_ref, ny, query.shape[0])
    coef, pos_coef = coefficients(query, noise, target, live_ref[...])
    send(msg_ref, ny, product(query, coef, NT), pos_coef * query)


def source_kernel(ny, reps, got_ref, et_ref, relt_ref, src_ref, rel_ref, live_ref, out_ref):
    query, relation = queries(et_ref, relt_ref, src_ref, rel_ref)
    features, rows = et_ref.shape
    fs, tiles = features // reps, rows // 128
    noise, target = received(got_ref, ny, features)
    coef, pos_coef = coefficients(query, noise, target, live_ref[...])
    grad = relation * (pos_coef * target + product(noise, coef))
    grad = pick(grad, one_hot(src_ref[...], rows), NT, 2)
    for r in range(reps):
        for t in range(tiles):
            at = (r * tiles + t) * fs
            out_ref[at : at + fs] = grad[r * fs : (r + 1) * fs, t * 128 : (t + 1) * 128]


def update_kernel(reps, grad_ref, et_ref, state_ref, entity_ref, new_state_ref):
    features, rows = et_ref.shape
    fs, tiles = features // reps, rows // 128
    for t in range(tiles):
        lanes = slice(t * 128, (t + 1) * 128)
        grads = [grad_ref[(r * tiles + t) * fs : (r * tiles + t + 1) * fs] for r in range(reps)]
        squares = sum(jnp.sum(grad * grad, axis=0, keepdims=True) for grad in grads)
        state = state_ref[:, lanes] + squares * (1.0 / features)
        new_state_ref[:, lanes] = state
        scale = LEARN_RATE / jnp.sqrt(state)
        for r, grad in enumerate(grads):
            at = slice(r * fs, (r + 1) * fs)
            entity_ref[at, lanes] = et_ref[at, lanes] - grad * scale


def floats(*shapes):
    return [(shape, F32) for shape in shapes]


def call(kernel, outs, *args, scratch=(), flops=0, inputs=pltpu.VMEM, outputs=pltpu.VMEM):
    make = pltpu.HBM if outputs == pltpu.HBM else jax.ShapeDtypeStruct
    shapes = [make(shape, dtype) for shape, dtype in outs]
    moved = sum(4 * a.size for a in args) + sum(4 * math.prod(shape) for shape, _ in outs)
    return pl.pallas_call(
        kernel,
        out_shape=shapes,
        in_specs=[pl.BlockSpec(memory_space=inputs)] * len(args),
        out_specs=[pl.BlockSpec(memory_space=outputs)] * len(outs),
        scratch_shapes=list(scratch),
        cost_estimate=pl.CostEstimate(flops=flops, bytes_accessed=moved, transcendentals=0),
        compiler_params=pltpu.CompilerParams(vmem_limit_bytes=48 << 20),
    )(*args)


def scatter_over_chips(blocks):
    reps = blocks.shape[0]
    chips = reps // 2
    me = lax.axis_index("rep")
    chip, core = me >> 1, me & 1
    pairs = blocks.reshape(chips, 2, *blocks.shape[1:])
    given = lax.dynamic_index_in_dim(pairs, 1 - core, 1, keepdims=False)
    kept = lax.dynamic_index_in_dim(pairs, core, 1, keepdims=False)
    kept = kept + lax.ppermute(given, "rep", [(i, i ^ 1) for i in range(reps)])
    total = lax.dynamic_index_in_dim(kept, chip, 0, keepdims=False)
    for step in range(1, chips):
        given = lax.dynamic_index_in_dim(kept, (chip + step) & (chips - 1), 0, keepdims=False)
        total = total + lax.ppermute(given, "rep", [(i, (i + 2 * step) % reps) for i in range(reps)])
    return total


def per_device(entity, adagrad_state, relation, src_rows, dst_rows, rel_ids, bucket_counts, noise_rows):
    nh, nl, ny, reps = (lax.axis_size(name) for name in ("h", "l", "y", "rep"))
    near = ("l", "y", "rep")
    devices = nl * ny * reps
    rows, features = entity.shape
    slots = src_rows.shape[3]
    edges = nh * nl * ny * slots
    fs, tiles = features // reps, rows // 128
    packed = tiles * fs

    et = entity.T
    mine = lax.dynamic_slice_in_dim(et, lax.axis_index("rep") * fs, fs, 0)
    table = lax.all_gather(mine.reshape(packed, 128), "h").reshape(nh * packed, 128)

    def turned(ids):
        return ids.reshape(nh * nl * ny, slots).T

    given = [turned(ids) for ids in (src_rows, rel_ids, dst_rows)]
    given += [noise_rows.reshape(1, edges), bucket_counts.reshape(1, -1)]
    row = ((1, edges), jnp.int32)
    src, rel, live, wanted = call(
        functools.partial(order_kernel, nh, nl, ny),
        [row, row, ((1, edges), F32), ((devices, 2 * nh * slots), jnp.int32)],
        *(pltpu.with_memory_space_constraint(a, pltpu.HBM) for a in given),
        scratch=[pltpu.VMEM(a.shape, a.dtype) for a in given] + [pltpu.SemaphoreType.DMA((len(given),))],
        inputs=pltpu.HBM,
    )
    asked = lax.all_to_all(wanted, near, split_axis=0, concat_axis=0, tiled=True)
    asked = asked.reshape(devices, 2, nh, slots).transpose(2, 1, 0, 3).reshape(nh, 1, -1)
    relt = relation.T

    unit = 2 * edges * features * rows
    span = 2 * nh * slots
    message = (devices * fs, span)
    wire = (devices, fs // 2, 2, span)
    held = round_up(fs, 8)
    got_shape = pltpu.VMEM((nh, held, 2 * devices * slots), F32)
    (found,) = call(
        functools.partial(table_kernel, fs),
        floats(message),
        table, asked,
        scratch=[got_shape, pltpu.VMEM((2 * held, rows), F32)],
        flops=8 * unit,
    )
    got = lax.all_to_all(found.reshape(wire), near, split_axis=0, concat_axis=0, tiled=True).reshape(message)
    edge_args = (got, et, relt, src, rel, live)
    (terms,) = call(functools.partial(terms_kernel, ny), floats(message), *edge_args, flops=11 * unit)
    terms = lax.all_to_all(terms.reshape(wire), near, split_axis=0, concat_axis=0, tiled=True).reshape(message)
    (partial,) = call(
        functools.partial(scatter_kernel, fs),
        floats((nh, packed, 128)),
        terms, asked,
        scratch=[got_shape, pltpu.VMEM((nh, packed, 128), F32), pltpu.SemaphoreType.DMA((nh,))],
        flops=8 * unit,
        outputs=pltpu.HBM,
    )
    (source,) = call(
        functools.partial(source_kernel, ny, reps), floats((reps * packed, 128)), *edge_args, flops=13 * unit
    )
    partial = lax.all_to_all(partial, "h", split_axis=0, concat_axis=0, tiled=True)
    grad = jnp.sum(partial, axis=0) + scatter_over_chips(source.reshape(reps, packed, 128))
    summed = lax.all_gather(grad, "rep").reshape(reps * packed, 128)
    new_entity, new_state = call(
        functools.partial(update_kernel, reps),
        floats((features, rows), (1, rows)),
        summed, et, adagrad_state.reshape(1, rows),
    )
    return new_entity.T, new_state.reshape(rows)


def solution(mesh):
    dom, reps = mesh.devices.shape
    ny = 4 if dom >= 16 else 2
    axes = ("h", "l", "y", "rep")
    cut = Mesh(mesh.devices.reshape(dom // (2 * ny), 2, ny, reps), axes)
    part = axes[:3]
    return jax.shard_map(
        per_device,
        mesh=cut,
        in_specs=(
            P(part, None),
            P(part),
            P(),
            P(part, "rep", None, None),
            P(part, "rep", None, None),
            P(part, "rep", None, None),
            P(part, "rep", None),
            P(part, "rep", None),
        ),
        out_specs=(P(part, None), P(part)),
        check_vma=False,
    )
```

```python
import functools
import math

import jax
import jax.numpy as jnp
from jax import lax
from jax.experimental import pallas as pl
from jax.experimental.pallas import tpu as pltpu
from jax.sharding import Mesh
from jax.sharding import PartitionSpec as P

LEARN_RATE = 0.3
F32 = jnp.float32
BF16 = jnp.bfloat16
NN = (((1,), (0,)), ((), ()))
NT = (((1,), (1,)), ((), ()))


def round_up(value, unit):
    return -(-value // unit) * unit


def one_hot(row, rows):
    place = lax.broadcasted_iota(jnp.int32, (rows, row.shape[1]), 0)
    return (place == row).astype(F32).astype(BF16)


def split(x, terms):
    out = []
    for _ in range(terms):
        part = x.astype(BF16)
        out.append(part)
        x = x - part.astype(F32)
    return out


def mul(a, b, dims=NN):
    return lax.dot_general(a, b, dims, preferred_element_type=F32)


def pick(x, hot, dims=NN, terms=2):
    n = x.shape[0]
    parts = [part.astype(F32) for part in split(x, terms)]
    out = mul(jnp.concatenate(parts, axis=0).astype(BF16), hot, dims)
    return sum(out[i * n : (i + 1) * n] for i in range(terms - 1, -1, -1))


def product(a, b, dims=NN):
    a_high, a_low = split(a, 2)
    b_high, b_low = split(b, 2)
    return mul(a_low, b_high, dims) + mul(a_high, b_low, dims) + mul(a_high, b_high, dims)


def skewed(v, block):
    n = len(v)
    k = 1
    while k < n:
        high = (block & k) != 0
        v = [jnp.where(high, v[(i + k) % n], v[i]) for i in range(n)]
        k *= 2
    return [v[-i % n] for i in range(n)]


def rotated(row, blocks, span, slots):
    parts = [row[:, i * span : (i + 1) * span] for i in range(row.shape[1] // span)]
    parts = [pltpu.roll(part, shift * slots, 1) if shift else part for part, shift in zip(parts, blocks)]
    return jnp.concatenate(parts, axis=1)


def turned_ids(ids_ref, h, nh, span, slots):
    row = ids_ref[h]
    each = row.shape[1] // (2 * span)
    return rotated(row, [kind * nh + h for kind in range(2) for _ in range(each)], span, slots)


def order_kernel(nh, nl, ny, *refs):
    given, (src_out, rel_out, live_out, wanted_ref), held, sems = refs[:5], refs[5:9], refs[9:14], refs[14]
    copies = [pltpu.make_async_copy(a, b, sems.at[i]) for i, (a, b) in enumerate(zip(given, held))]
    for copy in copies:
        copy.start()
    for copy in copies:
        copy.wait()
    src_ref, rel_ref, dst_ref, noise_ref, count_ref = held
    slots, parts = src_ref.shape
    edges = parts * slots
    lane = lax.broadcasted_iota(jnp.int32, (1, edges), 1)
    slot, group = lane % slots, lane // slots
    h, l, y = group % nh, group // nh % nl, group // (nh * nl)
    part = (h * nl + l) * ny + y
    here = one_hot(part, parts)
    stack = jnp.concatenate([src_ref[...], rel_ref[...], dst_ref[...]], axis=0).astype(F32)
    spread = pick(stack, here, terms=2)
    row = lax.broadcasted_iota(jnp.int32, (slots, edges), 0)

    def own(i):
        mine = jnp.where(row == slot, spread[i * slots : (i + 1) * slots], 0.0)
        return jnp.sum(mine, axis=0, keepdims=True).astype(jnp.int32)

    src_out[...] = own(0)
    rel_out[...] = own(1)
    target = own(2)
    wide = jnp.broadcast_to(noise_ref[...].astype(F32), (8, edges))
    noise = pick(wide, one_hot(part * slots + slot, edges), terms=2)[:1].astype(jnp.int32)
    wide = jnp.broadcast_to(count_ref[...].astype(F32), (8, parts))
    count = mul(wide.astype(BF16), here)[:1].astype(jnp.int32)
    live_out[...] = (slot < count).astype(F32)
    devices, span = wanted_ref.shape
    per = devices // (nl * ny)
    low = lax.broadcasted_iota(jnp.int32, (1, span), 1) < span // 2
    for i in range(ny):
        a, b = noise[:, i * span : (i + 1) * span], target[:, i * span : (i + 1) * span]
        first = jnp.where(low, a, pltpu.roll(b, span // 2, 1))
        second = jnp.where(low, pltpu.roll(a, span // 2, 1), b)
        for k, block in enumerate((first, second)):
            wanted_ref[(k * ny + i) * per : (k * ny + i + 1) * per] = jnp.broadcast_to(block, (per, span))


def queries(et_ref, relt_ref, src_ref, rel_ref):
    source = pick(et_ref[...], one_hot(src_ref[...], et_ref.shape[1]))
    relation = pick(relt_ref[...], one_hot(rel_ref[...], relt_ref.shape[1]))
    return source * relation, relation


def chunks(fs):
    return list(range(0, fs - 7, 8)) + ([fs - 8] if fs % 8 else [])


def table_kernel(fs, table_ref, ids_ref, out_ref, got_ref, stack_ref):
    nh, held, lanes = got_ref.shape
    span = out_ref.shape[1]
    devices = out_ref.shape[0] // fs
    tiles = table_ref.shape[0] // (nh * fs)
    n = 2 * nh
    slots = span // n
    terms = stack_ref.shape[0] // held

    for h in range(nh):
        for t in range(tiles):
            rows = table_ref[pl.ds(h * tiles * fs + t, fs, stride=tiles), :]
            for i, part in enumerate(split(rows, terms)):
                stack_ref[i * held : i * held + fs, t * 128 : (t + 1) * 128] = part.astype(F32)
        found = mul(stack_ref[...].astype(BF16), one_hot(turned_ids(ids_ref, h, nh, span, slots), tiles * 128))
        got_ref[h] = sum(found[i * held : (i + 1) * held] for i in range(terms - 1, -1, -1))
    block = lax.broadcasted_iota(jnp.int32, (8, span), 1) // slots

    def turn(tile, carry):
        for f in chunks(fs):
            v = []
            for kind in range(2):
                start = pl.multiple_of((kind * devices + tile * n) * slots, span)
                v += [got_ref[h, f : f + 8, pl.ds(start, span)] for h in range(nh)]
            v = skewed(v, block)
            for i in range(n):
                out_ref[pl.ds((tile * n + i) * fs + f, 8), :] = pltpu.roll(v[i], (n - i) % n * slots, 1) if i else v[i]
        return carry

    lax.fori_loop(0, devices // n, turn, 0)


def scatter_kernel(fs, msg_ref, ids_ref, out_ref, got_ref, sum_ref, sems):
    nh, held, lanes = got_ref.shape
    span = msg_ref.shape[1]
    devices = msg_ref.shape[0] // fs
    tiles = out_ref.shape[1] // fs
    n = 2 * nh
    slots = span // n
    block = lax.broadcasted_iota(jnp.int32, (8, span), 1) // slots

    def turn(tile, carry):
        for f in chunks(fs):
            v = [msg_ref[pl.ds((tile * n + i) * fs + f, 8), :] for i in range(n)]
            v = skewed([pltpu.roll(v[i], i * slots, 1) if i else v[i] for i in range(n)], block)
            for kind in range(2):
                start = pl.multiple_of((kind * devices + tile * n) * slots, span)
                for h in range(nh):
                    got_ref[h, f : f + 8, pl.ds(start, span)] = v[kind * nh + h]
        return carry

    lax.fori_loop(0, devices // n, turn, 0)

    copies = []
    for h in range(nh):
        grad = pick(got_ref[h], one_hot(turned_ids(ids_ref, h, nh, span, slots), tiles * 128), NT, 2)
        for t in range(tiles):
            sum_ref[h, t * fs : (t + 1) * fs] = grad[:fs, t * 128 : (t + 1) * 128]
        copies.append(pltpu.make_async_copy(sum_ref.at[h], out_ref.at[h], sems.at[h]))
        copies[-1].start()
    for copy in copies:
        copy.wait()


def received(got_ref, ny, features):
    span = got_ref.shape[1]
    low = lax.broadcasted_iota(jnp.int32, (1, span), 1) < span // 2
    noise, target = [], []
    for y in range(ny):
        first, second = (got_ref[(l * ny + y) * features : (l * ny + y + 1) * features] for l in range(2))
        noise.append(jnp.where(low, first, pltpu.roll(second, span // 2, 1)))
        target.append(jnp.where(low, pltpu.roll(first, span // 2, 1), second))
    return jnp.concatenate(noise, axis=1), jnp.concatenate(target, axis=1)


def send(msg_ref, ny, noise, target):
    features, span = noise.shape[0], msg_ref.shape[1]
    low = lax.broadcasted_iota(jnp.int32, (1, span), 1) < span // 2
    for y in range(ny):
        a, b = noise[:, y * span : (y + 1) * span], target[:, y * span : (y + 1) * span]
        first = jnp.where(low, a, pltpu.roll(b, span // 2, 1))
        second = jnp.where(low, pltpu.roll(a, span // 2, 1), b)
        for l, block in enumerate((first, second)):
            msg_ref[(l * ny + y) * features : (l * ny + y + 1) * features] = block


def coefficients(query, noise, target, live):
    coef = jax.nn.sigmoid(product(noise.T, query)) * live
    positive = jnp.sum(query * target, axis=0, keepdims=True)
    return coef, -jax.nn.sigmoid(-positive) * live


def terms_kernel(ny, got_ref, et_ref, relt_ref, src_ref, rel_ref, live_ref, msg_ref):
    query, _ = queries(et_ref, relt_ref, src_ref, rel_ref)
    noise, target = received(got_ref, ny, query.shape[0])
    coef, pos_coef = coefficients(query, noise, target, live_ref[...])
    send(msg_ref, ny, product(query, coef, NT), pos_coef * query)


def source_kernel(ny, reps, got_ref, et_ref, relt_ref, src_ref, rel_ref, live_ref, out_ref):
    query, relation = queries(et_ref, relt_ref, src_ref, rel_ref)
    features, rows = et_ref.shape
    fs, tiles = features // reps, rows // 128
    noise, target = received(got_ref, ny, features)
    coef, pos_coef = coefficients(query, noise, target, live_ref[...])
    grad = relation * (pos_coef * target + product(noise, coef))
    grad = pick(grad, one_hot(src_ref[...], rows), NT, 2)
    for r in range(reps):
        for t in range(tiles):
            at = (r * tiles + t) * fs
            out_ref[at : at + fs] = grad[r * fs : (r + 1) * fs, t * 128 : (t + 1) * 128]


def update_kernel(reps, grad_ref, et_ref, state_ref, entity_ref, new_state_ref):
    features, rows = et_ref.shape
    fs, tiles = features // reps, rows // 128
    for t in range(tiles):
        lanes = slice(t * 128, (t + 1) * 128)
        grads = [grad_ref[(r * tiles + t) * fs : (r * tiles + t + 1) * fs] for r in range(reps)]
        squares = sum(jnp.sum(grad * grad, axis=0, keepdims=True) for grad in grads)
        state = state_ref[:, lanes] + squares * (1.0 / features)
        new_state_ref[:, lanes] = state
        scale = LEARN_RATE / jnp.sqrt(state)
        for r, grad in enumerate(grads):
            at = slice(r * fs, (r + 1) * fs)
            entity_ref[at, lanes] = et_ref[at, lanes] - grad * scale


def floats(*shapes):
    return [(shape, F32) for shape in shapes]


def call(kernel, outs, *args, scratch=(), flops=0, inputs=pltpu.VMEM, outputs=pltpu.VMEM):
    make = pltpu.HBM if outputs == pltpu.HBM else jax.ShapeDtypeStruct
    shapes = [make(shape, dtype) for shape, dtype in outs]
    moved = sum(4 * a.size for a in args) + sum(4 * math.prod(shape) for shape, _ in outs)
    return pl.pallas_call(
        kernel,
        out_shape=shapes,
        in_specs=[pl.BlockSpec(memory_space=inputs)] * len(args),
        out_specs=[pl.BlockSpec(memory_space=outputs)] * len(outs),
        scratch_shapes=list(scratch),
        cost_estimate=pl.CostEstimate(flops=flops, bytes_accessed=moved, transcendentals=0),
        compiler_params=pltpu.CompilerParams(vmem_limit_bytes=48 << 20),
    )(*args)


def scatter_over_chips(blocks):
    reps = blocks.shape[0]
    chips = reps // 2
    me = lax.axis_index("rep")
    chip, core = me >> 1, me & 1
    pairs = blocks.reshape(chips, 2, *blocks.shape[1:])
    given = lax.dynamic_index_in_dim(pairs, 1 - core, 1, keepdims=False)
    kept = lax.dynamic_index_in_dim(pairs, core, 1, keepdims=False)
    kept = kept + lax.ppermute(given, "rep", [(i, i ^ 1) for i in range(reps)])
    total = lax.dynamic_index_in_dim(kept, chip, 0, keepdims=False)
    for step in range(1, chips):
        given = lax.dynamic_index_in_dim(kept, (chip + step) & (chips - 1), 0, keepdims=False)
        total = total + lax.ppermute(given, "rep", [(i, (i + 2 * step) % reps) for i in range(reps)])
    return total


def per_device(entity, adagrad_state, relation, src_rows, dst_rows, rel_ids, bucket_counts, noise_rows):
    nh, nl, ny, reps = (lax.axis_size(name) for name in ("h", "l", "y", "rep"))
    near = ("l", "y", "rep")
    devices = nl * ny * reps
    rows, features = entity.shape
    slots = src_rows.shape[3]
    edges = nh * nl * ny * slots
    fs, tiles = features // reps, rows // 128
    packed = tiles * fs

    et = entity.T
    mine = lax.dynamic_slice_in_dim(et, lax.axis_index("rep") * fs, fs, 0)
    table = lax.all_gather(mine.reshape(packed, 128), "h").reshape(nh * packed, 128)

    def turned(ids):
        return ids.reshape(nh * nl * ny, slots).T

    given = [turned(ids) for ids in (src_rows, rel_ids, dst_rows)]
    given += [noise_rows.reshape(1, edges), bucket_counts.reshape(1, -1)]
    row = ((1, edges), jnp.int32)
    src, rel, live, wanted = call(
        functools.partial(order_kernel, nh, nl, ny),
        [row, row, ((1, edges), F32), ((devices, 2 * nh * slots), jnp.int32)],
        *(pltpu.with_memory_space_constraint(a, pltpu.HBM) for a in given),
        scratch=[pltpu.VMEM(a.shape, a.dtype) for a in given] + [pltpu.SemaphoreType.DMA((len(given),))],
        inputs=pltpu.HBM,
    )
    asked = lax.all_to_all(wanted, near, split_axis=0, concat_axis=0, tiled=True)
    asked = asked.reshape(devices, 2, nh, slots).transpose(2, 1, 0, 3).reshape(nh, 1, -1)
    relt = relation.T

    unit = 2 * edges * features * rows
    span = 2 * nh * slots
    message = (devices * fs, span)
    wire = (devices, fs // 2, 2, span)
    held = round_up(fs, 8)
    got_shape = pltpu.VMEM((nh, held, 2 * devices * slots), F32)
    (found,) = call(
        functools.partial(table_kernel, fs),
        floats(message),
        table, asked,
        scratch=[got_shape, pltpu.VMEM((2 * held, rows), F32)],
        flops=8 * unit,
    )
    got = lax.all_to_all(found.reshape(wire), near, split_axis=0, concat_axis=0, tiled=True).reshape(message)
    edge_args = (got, et, relt, src, rel, live)
    (terms,) = call(functools.partial(terms_kernel, ny), floats(message), *edge_args, flops=11 * unit)
    terms = lax.all_to_all(terms.reshape(wire), near, split_axis=0, concat_axis=0, tiled=True).reshape(message)
    (partial,) = call(
        functools.partial(scatter_kernel, fs),
        floats((nh, packed, 128)),
        terms, asked,
        scratch=[got_shape, pltpu.VMEM((nh, packed, 128), F32), pltpu.SemaphoreType.DMA((nh,))],
        flops=8 * unit,
        outputs=pltpu.HBM,
    )
    (source,) = call(
        functools.partial(source_kernel, ny, reps), floats((reps * packed, 128)), *edge_args, flops=13 * unit
    )
    partial = lax.all_to_all(partial, "h", split_axis=0, concat_axis=0, tiled=True)
    grad = scatter_over_chips(source.reshape(reps, packed, 128)) + sum(partial[h] for h in range(nh))
    summed = lax.all_gather(grad, "rep").reshape(reps * packed, 128)
    new_entity, new_state = call(
        functools.partial(update_kernel, reps),
        floats((features, rows), (1, rows)),
        summed, et, adagrad_state.reshape(1, rows),
    )
    return new_entity.T, new_state.reshape(rows)


def solution(mesh):
    dom, reps = mesh.devices.shape
    ny = 4 if dom >= 16 else 2
    axes = ("h", "l", "y", "rep")
    cut = Mesh(mesh.devices.reshape(dom // (2 * ny), 2, ny, reps), axes)
    part = axes[:3]
    return jax.shard_map(
        per_device,
        mesh=cut,
        in_specs=(
            P(part, None),
            P(part),
            P(),
            P(part, "rep", None, None),
            P(part, "rep", None, None),
            P(part, "rep", None, None),
            P(part, "rep", None),
            P(part, "rep", None),
        ),
        out_specs=(P(part, None), P(part)),
        check_vma=False,
    )
```
